256 devices in a mesh: occ: 32 (over y, x, z_lo), vir: 8 (over z_hi, core).
Axes of the slice: x: 4, y: 4, z: 8 (z_hi: 4, z_lo: 2; z = z_hi * 2 + z_lo), core: 2. Of those that a mesh axis runs over, the one named last changes fastest.
Arguments:
- amplitudes: float32 [2304, 384, 384], P('occ', 'vir'), may hold values from -6 to 6
- integrals: float32 [384, 384, 1536], P('vir', 'occ'), may hold values from -0.015625 to 0.015625
Outputs:
- ladder: float32 [2304, 1536], P('occ', 'vir')
The draws below stay inside these ranges and needn't reach their ends.
All inputs are finite; a program needn't handle non-finite values.
Results may differ from the reference program's by a relative error of at most 0.000071.
Values sent between devices are 32-bit elements; how exact they have to be, the bound alone decides.
A program may use at most 128 MiB of HBM per device.

```python
import jax
import jax.numpy as jnp
from jax import lax

O = 48
V = 384
SLAB = 4
PAIRS = 2304


def levels(stream_key, extent, pieces, least, top_value):
    factor_of, own = 1.0, jax.random.fold_in(stream_key, 6)
    for axis_at, shards_of in pieces:
        heights = jnp.exp(jax.random.uniform(jax.random.fold_in(own, axis_at), (shards_of,), jnp.float32, least / len(pieces), top_value / len(pieces)))
        factor_of = factor_of * jnp.repeat(heights, extent[axis_at] // shards_of).reshape([-1 if axis == axis_at else 1 for axis in range(len(extent))])
    return factor_of


def centred(stream_key, dims, width, bound, shards=(), held_as=jnp.bfloat16):
    result = jax.random.normal(stream_key, dims, jnp.float32) * width
    if len(shards) > 0:
        result = levels(stream_key, dims, shards, -0.22, 0.18) * result
    return jnp.clip(result, min=-bound, max=bound).astype(held_as)


def setup_inputs(seed: int = 0) -> dict:
    keys = jax.random.split(jax.random.key(seed), 3)
    return {
        "amplitudes": centred(keys[0], (PAIRS, V, V), 1.0, 6.0, ((0, 32), (1, 8)), jnp.float32),
        "integrals": centred(keys[1], (V, V, SLAB * V), (V * V) ** -0.5, 0.015625, ((0, 8), (1, 32)), jnp.float32),
    }


def reference(amplitudes, integrals):
    grouped = amplitudes.reshape(O, O, V * V)
    symmetric = (grouped + jnp.transpose(grouped, (1, 0, 2))).reshape(PAIRS, V * V)
    slab_matrix = integrals.reshape(V * V, SLAB * V)
    return jnp.dot(symmetric, slab_matrix, precision=lax.Precision.HIGHEST, preferred_element_type=jnp.float32)
```

```python
import functools

import jax
import jax.numpy as jnp
from jax import lax
from jax.experimental import pallas as pl
from jax.experimental.pallas import tpu as pltpu
from jax.sharding import PartitionSpec as P

O = 48
MESH = pl.DeviceIdType.MESH
F32, BF16 = jnp.float32, jnp.bfloat16
SIZE = {"y": 4, "x": 4, "z": 2}
AXIS = {"y": 0, "x": 1, "z": 2}
ORDERS = (("y", "x", "z"), ("x", "z", "y"), ("z", "y", "x"))
ROWS, DEPTH, WIDE, COLS = 72, 576, 640, 1536
PAIRS = 2304


def occ_place():
    r = lax.axis_index("occ")
    return {"y": r // 8, "x": lax.rem(r // 2, 4), "z": lax.rem(r, 2)}


def occ_peer(me, dim, k):
    c = dict(me)
    c[dim] = lax.rem(me[dim] + k, SIZE[dim])
    return c[dim], c["y"] * 8 + c["x"] * 2 + c["z"]


def exchange_kernel(x_ref, o_ref, g1, g2, ssem, rsem, lsem):
    v = lax.axis_index("vir")
    me = occ_place()
    third = ROWS // 3
    barrier = pltpu.get_barrier_semaphore()
    for dim in "yxz":
        for k in range(1, SIZE[dim]):
            pl.semaphore_signal(barrier, inc=1, device_id=(occ_peer(me, dim, k)[1], v), device_id_type=MESH)
    pl.semaphore_wait(barrier, 7)

    def view(ref, t, dim, at, whole):
        ix = [slice(None)] * 3
        ix[AXIS[dim]] = at
        if whole:
            return ref.at[ix[0], ix[1], ix[2], pl.ds(t * third, third)]
        return ref.at[t, ix[0], ix[1], ix[2]]

    held = [(x_ref, True), (g1, False), (g2, False), (o_ref, True)]

    def start(t, s):
        dim = ORDERS[t][s]
        (src, src_whole), (dst, dst_whole) = held[s], held[s + 1]
        copies = []
        for k in range(1, SIZE[dim]):
            at, rank = occ_peer(me, dim, k)
            copies.append(
                pltpu.make_async_remote_copy(
                    src_ref=view(src, t, dim, at, src_whole),
                    dst_ref=view(dst, t, dim, me[dim], dst_whole),
                    send_sem=ssem.at[t, s, k - 1],
                    recv_sem=rsem.at[t, s, k - 1],
                    device_id=(rank, v),
                    device_id_type=MESH,
                )
            )
        copies.append(
            pltpu.make_async_copy(
                view(src, t, dim, me[dim], src_whole), view(dst, t, dim, me[dim], dst_whole), lsem.at[t, s]
            )
        )
        for c in copies:
            c.start()
        return copies

    flying = [start(t, 0) for t in range(3)]
    for s in (1, 2, 3):
        following = []
        for t in range(3):
            for c in flying[t]:
                c.wait()
            if s < 3:
                following.append(start(t, s))
        flying = following


def exchange(x):
    return pl.pallas_call(
        exchange_kernel,
        out_shape=jax.ShapeDtypeStruct((4, 4, 2, ROWS, WIDE), F32),
        in_specs=[pl.BlockSpec(memory_space=pl.ANY)],
        out_specs=pl.BlockSpec(memory_space=pl.ANY),
        scratch_shapes=[
            pltpu.VMEM((3, 4, 4, 2, ROWS // 3, WIDE), F32),
            pltpu.VMEM((3, 4, 4, 2, ROWS // 3, WIDE), F32),
            pltpu.SemaphoreType.DMA((3, 3, 3)),
            pltpu.SemaphoreType.DMA((3, 3, 3)),
            pltpu.SemaphoreType.DMA((3, 3)),
        ],
        compiler_params=pltpu.CompilerParams(collective_id=0, has_side_effects=True, vmem_limit_bytes=40 << 20),
    )(x)


def split(x):
    hi = x.astype(BF16)
    return hi, (x - hi.astype(F32)).astype(BF16)


def product_kernel(a_any, b_ref, c_ref, a_ref, s_hi, s_lo, b_hi, b_lo, sem):
    n = pl.program_id(0)

    @pl.when(n == 0)
    def _():
        tiles = WIDE // 128
        copies = [
            pltpu.make_async_copy(a_any.at[:, pl.ds(t * 128, 128)], a_ref.at[t], sem.at[t]) for t in range(tiles)
        ]
        for c in copies:
            c.start()

        @pl.loop(0, DEPTH // 48)
        def _(k):
            rows = pl.ds(pl.multiple_of(k * 48, 16), 48)
            b = b_ref[rows, :]
            for core in range(2):
                for h in range(2):
                    at = [(2 * h + e) * 384 + core * 192 for e in range(2)]
                    piece = jnp.concatenate([b[:, q : q + 192] for q in at], axis=1)
                    b_hi[core * 2 + h, rows, :], b_lo[core * 2 + h, rows, :] = split(piece)

        for t in range(tiles):
            copies[t].wait()

            @pl.loop(0, O)
            def _(i):
                rows = pl.ds(pl.multiple_of(i * O, 16), O)
                w = min(128, DEPTH - t * 128)
                s = a_ref[t, rows, :] + a_ref[t, pl.ds(i, O, stride=O), :]
                lanes = slice(t * 128, t * 128 + w)
                s_hi[rows, lanes], s_lo[rows, lanes] = split(s[:, :w])

    @pl.loop(0, PAIRS // 256)
    def _(m):
        rows = pl.ds(pl.multiple_of(m * 256, 256), 256)
        dot = functools.partial(jnp.dot, preferred_element_type=F32)
        c_ref[0, rows, :] = (
            dot(s_hi[rows, :], b_lo[n]) + dot(s_lo[rows, :], b_hi[n]) + dot(s_hi[rows, :], b_hi[n])
        )


def product(a, b):
    return pl.pallas_call(
        product_kernel,
        grid=(4,),
        out_shape=jax.ShapeDtypeStruct((4, PAIRS, 384), F32),
        in_specs=[pl.BlockSpec(memory_space=pl.ANY), pl.BlockSpec(memory_space=pltpu.VMEM)],
        out_specs=pl.BlockSpec((1, PAIRS, 384), lambda n: (n, 0, 0)),
        scratch_shapes=[
            pltpu.VMEM((WIDE // 128, PAIRS, 128), F32),
            pltpu.VMEM((PAIRS, DEPTH), BF16),
            pltpu.VMEM((PAIRS, DEPTH), BF16),
            pltpu.VMEM((4, DEPTH, 384), BF16),
            pltpu.VMEM((4, DEPTH, 384), BF16),
            pltpu.SemaphoreType.DMA((WIDE // 128,)),
        ],
        compiler_params=pltpu.CompilerParams(vmem_limit_bytes=48 << 20),
        cost_estimate=pl.CostEstimate(flops=6 * PAIRS * DEPTH * COLS, bytes_accessed=24 << 20, transcendentals=0),
    )(a, b)


def reduce_kernel(c_ref, o_ref, acc, other, r1, s1, r2, s2, r3, ssem, rsem, lsem):
    v = lax.axis_index("vir")
    core, zh = lax.rem(v, 2), v // 2
    me = occ_place()
    r = lax.axis_index("occ")
    zl = me["z"]
    barrier = pltpu.get_barrier_semaphore()

    def line(k):
        z = lax.rem(zh * 2 + zl + k, 8)
        zl_to, zh_to = lax.rem(z, 2), z // 2
        return zl_to, zh_to, (r - zl + zl_to, zh_to * 2 + core)

    twin = (r, v + 1 - 2 * core)
    devices = [twin] + [(occ_peer(me, dim, k)[1], v) for dim in "yx" for k in range(1, 4)]
    devices += [line(k)[2] for k in range(1, 8)]
    for d in devices:
        pl.semaphore_signal(barrier, inc=1, device_id=d, device_id_type=MESH)
    pl.semaphore_wait(barrier, len(devices))

    def remote(n, src, dst, device):
        c = pltpu.make_async_remote_copy(
            src_ref=src, dst_ref=dst, send_sem=ssem.at[n], recv_sem=rsem.at[n], device_id=device, device_id_type=MESH
        )
        c.start()
        return c

    own = [pltpu.make_async_copy(c_ref.at[core * 2 + h], acc.at[h], lsem.at[h]) for h in range(2)]
    for c in own:
        c.start()
    swap = [remote(h, c_ref.at[(1 - core) * 2 + h], other.at[h], twin) for h in range(2)]
    first = []
    for h in range(2):
        own[h].wait()
        swap[h].wait()

        @pl.loop(0, PAIRS // 72)
        def _(m):
            rows = pl.ds(pl.multiple_of(m * 72, 8), 72)
            acc[h, rows, :] += other[h, rows, :]

        dim = "yx"[h]
        for k in range(1, 4):
            at, rank = occ_peer(me, dim, k)
            rows = pl.ds(pl.multiple_of(at * 576, 8), 576)
            if h == 0:
                first.append(remote(2 + k - 1, acc.at[0, rows], r1.at[0, k - 1], (rank, v)))
            else:
                for y in range(4):
                    rows = pl.ds(pl.multiple_of(y * 576 + at * 144, 8), 144)
                    first.append(
                        remote(5 + (k - 1) * 4 + y, acc.at[1, rows], r1.at[1, k - 1, pl.ds(y * 144, 144)], (rank, v))
                    )

    second = []
    for h in range(2):
        for c in first[:3] if h == 0 else first[3:]:
            c.wait()
        for y in range(4):
            part = pl.ds(y * 144, 144)
            base = (me["y"] * 576 + y * 144) if h == 0 else (y * 576 + me["x"] * 144)
            mine = pl.ds(pl.multiple_of(base, 8), 144)
            s1[h, part, :] = (acc[h, mine, :] + r1[h, 0, part, :]) + (r1[h, 1, part, :] + r1[h, 2, part, :])
        dim = "xy"[h]
        for k in range(1, 4):
            at, rank = occ_peer(me, dim, k)
            rows = pl.ds(pl.multiple_of(at * 144, 8), 144)
            second.append(remote(17 + h * 3 + k - 1, s1.at[h, rows], r2.at[h, k - 1], (rank, v)))

    for h in range(2):
        for c in second[3 * h : 3 * h + 3]:
            c.wait()
        mine = pl.ds(pl.multiple_of(me["xy"[h]] * 144, 8), 144)
        s2[h] = (s1[h, mine, :] + r2[h, 0]) + (r2[h, 1] + r2[h, 2])

    def part(zl_to, zh_to):
        rows = pl.ds(pl.multiple_of(zl_to * 72, 8), 72)
        lanes = pl.ds(pl.multiple_of(lax.rem(zh_to, 2) * 128, 128), 256)
        return s2.at[zh_to // 2, rows, lanes]

    third = []
    for k in range(1, 8):
        zl_to, zh_to, device = line(k)
        third.append(remote(23 + k - 1, part(zl_to, zh_to), r3.at[k - 1], device))
    total = part(zl, zh)[...]
    for k in range(1, 8):
        third[k - 1].wait()
        total += r3[k - 1]
    o_ref[...] = jnp.where(lax.rem(zh, 2) == 0, total[:, :192], total[:, 64:])


def reduce(c):
    return pl.pallas_call(
        reduce_kernel,
        out_shape=jax.ShapeDtypeStruct((ROWS, 192), F32),
        in_specs=[pl.BlockSpec(memory_space=pl.ANY)],
        out_specs=pl.BlockSpec(memory_space=pltpu.VMEM),
        scratch_shapes=[
            pltpu.VMEM((2, PAIRS, 384), F32),
            pltpu.VMEM((2, PAIRS, 384), F32),
            pltpu.VMEM((2, 3, 576, 384), F32),
            pltpu.VMEM((2, 576, 384), F32),
            pltpu.VMEM((2, 3, 144, 384), F32),
            pltpu.VMEM((2, 144, 384), F32),
            pltpu.VMEM((7, ROWS, 256), F32),
            pltpu.SemaphoreType.DMA((30,)),
            pltpu.SemaphoreType.DMA((30,)),
            pltpu.SemaphoreType.DMA((2,)),
        ],
        compiler_params=pltpu.CompilerParams(collective_id=1, has_side_effects=True, vmem_limit_bytes=48 << 20),
    )(c)


def on_device(amplitudes, integrals):
    slabs = amplitudes.reshape(ROWS, O, 32, 12).transpose(2, 0, 3, 1).reshape(4, 4, 2, ROWS, DEPTH)
    slabs = jnp.pad(slabs, ((0, 0),) * 4 + ((0, WIDE - DEPTH),))
    columns = exchange(slabs).reshape(PAIRS, WIDE)
    slab_matrix = integrals.transpose(1, 0, 2).reshape(DEPTH, COLS)
    return reduce(product(columns, slab_matrix))


def solution(mesh):
    in_specs = (P("occ", "vir", None), P("vir", "occ", None))
    out_specs = P("occ", "vir")
    return jax.shard_map(
        on_device, mesh=mesh, in_specs=in_specs, out_specs=out_specs, check_vma=False
    )
```

```python
import functools

import jax
import jax.numpy as jnp
from jax import lax
from jax.experimental import pallas as pl
from jax.experimental.pallas import tpu as pltpu
from jax.sharding import PartitionSpec as P

O = 48
MESH = pl.DeviceIdType.MESH
F32, BF16 = jnp.float32, jnp.bfloat16
SIZE = {"y": 4, "x": 4, "z": 2}
AXIS = {"y": 0, "x": 1, "z": 2}
ORDERS = (("y", "x", "z"), ("x", "z", "y"), ("z", "y", "x"))
ROWS, DEPTH, WIDE, COLS = 72, 576, 640, 1536
PAIRS = 2304


def occ_place():
    r = lax.axis_index("occ")
    return {"y": r // 8, "x": lax.rem(r // 2, 4), "z": lax.rem(r, 2)}


def occ_peer(me, dim, k):
    c = dict(me)
    c[dim] = lax.rem(me[dim] + k, SIZE[dim])
    return c[dim], c["y"] * 8 + c["x"] * 2 + c["z"]


def exchange_kernel(x_ref, o_ref, g1, g2, ssem, rsem, lsem):
    v = lax.axis_index("vir")
    me = occ_place()
    third = ROWS // 3
    barrier = pltpu.get_barrier_semaphore()
    for dim in "yxz":
        for k in range(1, SIZE[dim]):
            pl.semaphore_signal(barrier, inc=1, device_id=(occ_peer(me, dim, k)[1], v), device_id_type=MESH)
    pl.semaphore_wait(barrier, 7)

    def view(ref, t, dim, at, whole):
        ix = [slice(None)] * 3
        ix[AXIS[dim]] = at
        if whole:
            return ref.at[ix[0], ix[1], ix[2], pl.ds(t * third, third)]
        return ref.at[t, ix[0], ix[1], ix[2]]

    held = [(x_ref, True), (g1, False), (g2, False), (o_ref, True)]

    def start(t, s):
        dim = ORDERS[t][s]
        (src, src_whole), (dst, dst_whole) = held[s], held[s + 1]
        copies = []
        for k in range(1, SIZE[dim]):
            at, rank = occ_peer(me, dim, k)
            copies.append(
                pltpu.make_async_remote_copy(
                    src_ref=view(src, t, dim, at, src_whole),
                    dst_ref=view(dst, t, dim, me[dim], dst_whole),
                    send_sem=ssem.at[t, s, k - 1],
                    recv_sem=rsem.at[t, s, k - 1],
                    device_id=(rank, v),
                    device_id_type=MESH,
                )
            )
        copies.append(
            pltpu.make_async_copy(
                view(src, t, dim, me[dim], src_whole), view(dst, t, dim, me[dim], dst_whole), lsem.at[t, s]
            )
        )
        for c in copies:
            c.start()
        return copies

    flying = [start(t, 0) for t in range(3)]
    for s in (1, 2, 3):
        following = []
        for t in range(3):
            for c in flying[t]:
                c.wait()
            if s < 3:
                following.append(start(t, s))
        flying = following


def exchange(x):
    return pl.pallas_call(
        exchange_kernel,
        out_shape=jax.ShapeDtypeStruct((4, 4, 2, ROWS, WIDE), F32),
        in_specs=[pl.BlockSpec(memory_space=pl.ANY)],
        out_specs=pl.BlockSpec(memory_space=pl.ANY),
        scratch_shapes=[
            pltpu.VMEM((3, 4, 4, 2, ROWS // 3, WIDE), F32),
            pltpu.VMEM((3, 4, 4, 2, ROWS // 3, WIDE), F32),
            pltpu.SemaphoreType.DMA((3, 3, 3)),
            pltpu.SemaphoreType.DMA((3, 3, 3)),
            pltpu.SemaphoreType.DMA((3, 3)),
        ],
        compiler_params=pltpu.CompilerParams(collective_id=0, has_side_effects=True, vmem_limit_bytes=40 << 20),
    )(x)


def split(x):
    hi = x.astype(BF16)
    return hi, (x - hi.astype(F32)).astype(BF16)


TURN = (2, 0, 1)
KEPT = 80
UNIQUE = 16 * KEPT


def runs(start, count, *stops):
    out = []
    while count:
        start %= O
        n = min([count, O - start] + [p - start for p in stops if p > start])
        out.append((start, n))
        start, count = start + n, count - n
    return out


def pair_sum_kernel(a_any, hi_ref, lo_ref, a_ref, sem):
    tiles = WIDE // 128
    copies = [pltpu.make_async_copy(a_any.at[:, pl.ds(t * 128, 128)], a_ref.at[t], sem.at[t]) for t in range(tiles)]
    for c in copies:
        c.start()
    for t in range(tiles):
        copies[t].wait()
        for q in range(16):
            rows = []
            for k in range(3):
                i, m = 3 * q + TURN[k], int(k == 0)
                rows += [
                    a_ref[t, i * O + j : i * O + j + n, :] + a_ref[t, pl.ds(j * O + i, n, stride=O), :]
                    for j, n in runs(3 * q + m, 27 - m)
                ]
            at, lanes = slice(q * KEPT, (q + 1) * KEPT), slice(t * 128, (t + 1) * 128)
            hi_ref[at, lanes], lo_ref[at, lanes] = split(jnp.concatenate(rows, axis=0))


def pair_sum(a):
    return pl.pallas_call(
        pair_sum_kernel,
        out_shape=[jax.ShapeDtypeStruct((UNIQUE, WIDE), BF16)] * 2,
        in_specs=[pl.BlockSpec(memory_space=pl.ANY)],
        out_specs=[pl.BlockSpec(memory_space=pltpu.VMEM)] * 2,
        scratch_shapes=[
            pltpu.VMEM((WIDE // 128, PAIRS, 128), F32),
            pltpu.SemaphoreType.DMA((WIDE // 128,)),
        ],
        compiler_params=pltpu.CompilerParams(vmem_limit_bytes=24 << 20),
    )(a)


def ladder_kernel(
    hi_ref, lo_ref, b_ref, o_ref, b_hi, b_lo, away, acc, other, r1, s1, r2, s2, r3, mine, r4, ends, r5, ssem, rsem
):
    v = lax.axis_index("vir")
    core, zh = lax.rem(v, 2), v // 2
    me = occ_place()
    r = lax.axis_index("occ")
    q, zl = r // 2, me["z"]
    barrier = pltpu.get_barrier_semaphore()

    def triple(k):
        return (lax.rem(q + k, 16) * 2 + zl, v)

    def high(k):
        to = lax.rem(zh + k, 4)
        return to, (r, to * 2 + core)

    twin = (r, v + 1 - 2 * core)
    beside = (r + 1 - 2 * zl, v)
    devices = [twin, beside] + [triple(k) for k in range(1, 16)] + [high(k)[1] for k in range(1, 4)]
    for d in devices:
        pl.semaphore_signal(barrier, inc=1, device_id=d, device_id_type=MESH)

    sent = [0]

    def remote(src, dst, device):
        n = sent[0]
        sent[0] += 1
        c = pltpu.make_async_remote_copy(
            src_ref=src, dst_ref=dst, send_sem=ssem.at[n], recv_sem=rsem.at[n], device_id=device, device_id_type=MESH
        )
        c.start()
        return c

    @pl.loop(0, DEPTH // 48)
    def _(k):
        rows = pl.ds(pl.multiple_of(k * 48, 16), 48)
        b = b_ref[rows, :]
        for c in range(2):
            for h in range(2):
                at = [(2 * h + e) * 384 + c * 192 for e in range(2)]
                piece = jnp.concatenate([b[:, p : p + 192] for p in at], axis=1)
                b_hi[c * 2 + h, rows, :], b_lo[c * 2 + h, rows, :] = split(piece)

    def product(n, out, h):
        @pl.loop(0, UNIQUE // 256)
        def _(m):
            rows = pl.ds(pl.multiple_of(m * 256, 256), 256)
            dot = functools.partial(jnp.dot, preferred_element_type=F32)
            hi, lo = hi_ref[rows, :DEPTH], lo_ref[rows, :DEPTH]
            out[h, rows, :] = dot(hi, b_lo[n]) + dot(lo, b_hi[n]) + dot(hi, b_hi[n])

    swap = []
    for h in range(2):
        product((1 - core) * 2 + h, away, h)
        if h == 0:
            pl.semaphore_wait(barrier, len(devices))
        swap.append(remote(away.at[h], other.at[h], twin))

    first = [[], []]
    for h in range(2):
        product(core * 2 + h, acc, h)
        swap[h].wait()

        @pl.loop(0, 16)
        def _(m):
            rows = pl.ds(pl.multiple_of(m * KEPT, 8), KEPT)
            acc[h, rows, :] += other[h, rows, :]

        dim = "yx"[h]
        for k in range(1, 4):
            at, rank = occ_peer(me, dim, k)
            if h == 0:
                rows = pl.ds(pl.multiple_of(at * 4 * KEPT, 8), 4 * KEPT)
                first[h].append(remote(acc.at[h, rows], r1.at[h, k - 1], (rank, v)))
            else:
                for y in range(4):
                    rows = pl.ds(pl.multiple_of((y * 4 + at) * KEPT, 8), KEPT)
                    first[h].append(remote(acc.at[h, rows], r1.at[h, k - 1, pl.ds(y * KEPT, KEPT)], (rank, v)))

    second = [[], []]
    for h in range(2):
        for c in first[h]:
            c.wait()
        for y in range(4):
            part = pl.ds(y * KEPT, KEPT)
            base = (me["y"] * 4 + y) if h == 0 else (y * 4 + me["x"])
            own = pl.ds(pl.multiple_of(base * KEPT, 8), KEPT)
            s1[h, part, :] = (acc[h, own, :] + r1[h, 0, part, :]) + (r1[h, 1, part, :] + r1[h, 2, part, :])
        for k in range(1, 4):
            at, rank = occ_peer(me, "xy"[h], k)
            rows = pl.ds(pl.multiple_of(at * KEPT, 8), KEPT)
            second[h].append(remote(s1.at[h, rows], r2.at[h, k - 1], (rank, v)))

    for h in range(2):
        for c in second[h]:
            c.wait()
        own = pl.ds(pl.multiple_of(me["xy"[h]] * KEPT, 8), KEPT)
        s2[h] = (s1[h, own, :] + r2[h, 0]) + (r2[h, 1] + r2[h, 2])

    def part(to):
        return s2.at[to // 2, :, pl.ds(pl.multiple_of(lax.rem(to, 2) * 128, 128), 256)]

    third = [remote(part(high(k)[0]), r3.at[k - 1], high(k)[1]) for k in range(1, 4)]
    total = part(zh)[...]
    for k in range(1, 4):
        third[k - 1].wait()
        total += r3[k - 1]
    mine[...] = jnp.where(lax.rem(zh, 2) == 0, total[:, :192], total[:, 64:])
    fourth = remote(mine, r4, beside)
    fourth.wait()
    u = mine[...] + r4[...]

    def kept(k, m):
        return u[27 * k - 1 + m : 27 * k + m]

    fifth = []
    for k in range(1, 8):
        ends[k - 1, :9] = jnp.concatenate([kept(e, 3 * k + t) for t in range(3) for e in (1, 2, 0)], axis=0)
        fifth.append(remote(ends.at[k - 1], r5.at[k - 1], triple(k)))
    for c in fifth:
        c.wait()
    turned = []
    for t in range(3):
        k = TURN.index(t)
        rows = [u[27 * k - 1 : 27 * k + 26]] if k else [kept(1, 2), u[0:26]]
        rows += [r5[6 - e, 3 * t : 3 * t + 3] for e in range(7)]
        turned.append(pltpu.roll(jnp.concatenate(rows, axis=0), 3 * q, 0))
    low = jnp.concatenate([turned[0], turned[1][:24]], axis=0)
    top = jnp.concatenate([turned[1][24:], turned[2]], axis=0)
    o_ref[...] = jnp.where(zl == 0, low, top)


def ladder(hi, lo, b):
    return pl.pallas_call(
        ladder_kernel,
        out_shape=jax.ShapeDtypeStruct((ROWS, 192), F32),
        in_specs=[pl.BlockSpec(memory_space=pltpu.VMEM)] * 3,
        out_specs=pl.BlockSpec(memory_space=pltpu.VMEM),
        scratch_shapes=[
            pltpu.VMEM((4, DEPTH, 384), BF16),
            pltpu.VMEM((4, DEPTH, 384), BF16),
            pltpu.VMEM((2, UNIQUE, 384), F32),
            pltpu.VMEM((2, UNIQUE, 384), F32),
            pltpu.VMEM((2, UNIQUE, 384), F32),
            pltpu.VMEM((2, 3, 4 * KEPT, 384), F32),
            pltpu.VMEM((2, 4 * KEPT, 384), F32),
            pltpu.VMEM((2, 3, KEPT, 384), F32),
            pltpu.VMEM((2, KEPT, 384), F32),
            pltpu.VMEM((3, KEPT, 256), F32),
            pltpu.VMEM((KEPT, 192), F32),
            pltpu.VMEM((KEPT, 192), F32),
            pltpu.VMEM((7, 16, 192), F32),
            pltpu.VMEM((7, 16, 192), F32),
            pltpu.SemaphoreType.DMA((34,)),
            pltpu.SemaphoreType.DMA((34,)),
        ],
        compiler_params=pltpu.CompilerParams(collective_id=1, has_side_effects=True, vmem_limit_bytes=48 << 20),
    )(hi, lo, b)


def on_device(amplitudes, integrals):
    slabs = amplitudes.reshape(ROWS, O, 32, 12).transpose(2, 0, 3, 1).reshape(4, 4, 2, ROWS, DEPTH)
    slabs = jnp.pad(slabs, ((0, 0),) * 4 + ((0, WIDE - DEPTH),))
    columns = exchange(slabs).reshape(PAIRS, WIDE)
    slab_matrix = integrals.transpose(1, 0, 2).reshape(DEPTH, COLS)
    return ladder(*pair_sum(columns), slab_matrix)


def solution(mesh):
    in_specs = (P("occ", "vir", None), P("vir", "occ", None))
    out_specs = P("occ", "vir")
    return jax.shard_map(
        on_device, mesh=mesh, in_specs=in_specs, out_specs=out_specs, check_vma=False
    )
```

```python
import functools

import jax
import jax.numpy as jnp
from jax import lax
from jax.experimental import pallas as pl
from jax.experimental.pallas import tpu as pltpu
from jax.sharding import PartitionSpec as P

O = 48
MESH = pl.DeviceIdType.MESH
F32, BF16 = jnp.float32, jnp.bfloat16
SIZE = {"y": 4, "x": 4, "z": 2}
AXIS = {"y": 0, "x": 1, "z": 2}
ORDERS = (("y", "x", "z"), ("x", "z", "y"), ("z", "y", "x"))
ROWS, DEPTH, WIDE, COLS = 72, 576, 640, 1536
PAIRS = 2304


def occ_place():
    r = lax.axis_index("occ")
    return {"y": r // 8, "x": lax.rem(r // 2, 4), "z": lax.rem(r, 2)}


def occ_peer(me, dim, k):
    c = dict(me)
    c[dim] = lax.rem(me[dim] + k, SIZE[dim])
    return c[dim], c["y"] * 8 + c["x"] * 2 + c["z"]


THIRD = ROWS // 3
SLAB = 4 * THIRD + 16
PITCH = 392


def exchange_kernel(x_ref, o_ref, x, turned, g0, g1, g2, ssem, rsem, lsem, xsem):
    v = lax.axis_index("vir")
    me = occ_place()
    reads = [pltpu.make_async_copy(x_ref.at[pl.ds(t * THIRD, THIRD)], x.at[t], xsem.at[t]) for t in range(3)]
    for c in reads:
        c.start()
    barrier = pltpu.get_barrier_semaphore()
    for dim in "yxz":
        for k in range(1, SIZE[dim]):
            pl.semaphore_signal(barrier, inc=1, device_id=(occ_peer(me, dim, k)[1], v), device_id_type=MESH)

    lane = lax.broadcasted_iota(jnp.int32, (8, 128), 1)

    def regroup(t, block):
        @pl.loop(0, 8, unroll=8)
        def _(p):
            turned[pl.ds(pl.multiple_of(p * PITCH, 8), 384), 0:O] = x[t, block * 8 + p].T

        @pl.loop(0, 32, unroll=8)
        def _(to):
            at = (t, to // 8, lax.rem(to // 2, 4), lax.rem(to, 2))
            tiles = [jnp.zeros((8, 128), F32)] * 5
            for d in range(12):
                tile, off = d * O // 128, d * O % 128
                piece = turned[pl.ds(to * 12 + d, 8, stride=PITCH), :]
                if off:
                    piece = pltpu.roll(piece, off, 1)
                tiles[tile] = jnp.where((lane >= off) & (lane < off + O), piece, tiles[tile])
                if off + O > 128:
                    tiles[tile + 1] = jnp.where(lane < off + O - 128, piece, tiles[tile + 1])
            for n in range(4):
                g0[(*at, slice(n * THIRD + block * 8, n * THIRD + block * 8 + 8))] = tiles[n]
            rest = (*at, slice(4 * THIRD + block // 2 * 8, 4 * THIRD + block // 2 * 8 + 8))
            if block == 1:
                g0[rest] = jnp.where(lane < 64, g0[rest], pltpu.roll(tiles[4], 64, 1))
            else:
                g0[rest] = tiles[4]

    def view(ref, t, dim, at):
        ix = [slice(None)] * 3
        ix[AXIS[dim]] = at
        if ref is o_ref:
            return ref.at[ix[0], ix[1], ix[2], t]
        return ref.at[t, ix[0], ix[1], ix[2]]

    held = [g0, g1, g2, o_ref]

    def start(t, s):
        dim = ORDERS[t][s]
        src, dst = held[s], held[s + 1]
        copies = []
        for k in range(1, SIZE[dim]):
            at, rank = occ_peer(me, dim, k)
            copies.append(
                pltpu.make_async_remote_copy(
                    src_ref=view(src, t, dim, at),
                    dst_ref=view(dst, t, dim, me[dim]),
                    send_sem=ssem.at[t, s, k - 1],
                    recv_sem=rsem.at[t, s, k - 1],
                    device_id=(rank, v),
                    device_id_type=MESH,
                )
            )
        copies.append(
            pltpu.make_async_copy(view(src, t, dim, me[dim]), view(dst, t, dim, me[dim]), lsem.at[t, s])
        )
        for c in copies:
            c.start()
        return copies

    flying = []
    for t in range(3):
        reads[t].wait()
        for block in range(3):
            regroup(t, block)
        if t == 0:
            pl.semaphore_wait(barrier, 7)
        flying.append(start(t, 0))
    for s in (1, 2, 3):
        following = []
        for t in range(3):
            for c in flying[t]:
                c.wait()
            if s < 3:
                following.append(start(t, s))
        flying = following


def exchange(x):
    slabs = pltpu.VMEM((3, 4, 4, 2, SLAB, 128), F32)
    return pl.pallas_call(
        exchange_kernel,
        out_shape=jax.ShapeDtypeStruct((4, 4, 2, 3, SLAB, 128), F32),
        in_specs=[pl.BlockSpec(memory_space=pl.ANY)],
        out_specs=pl.BlockSpec(memory_space=pl.ANY),
        scratch_shapes=[
            pltpu.VMEM((3, THIRD, O, 384), F32),
            pltpu.VMEM((8 * PITCH, 128), F32),
            slabs,
            slabs,
            slabs,
            pltpu.SemaphoreType.DMA((3, 3, 3)),
            pltpu.SemaphoreType.DMA((3, 3, 3)),
            pltpu.SemaphoreType.DMA((3, 3)),
            pltpu.SemaphoreType.DMA((3,)),
        ],
        compiler_params=pltpu.CompilerParams(collective_id=0, has_side_effects=True, vmem_limit_bytes=52 << 20),
    )(x)


def split(x):
    hi = x.astype(BF16)
    return hi, (x - hi.astype(F32)).astype(BF16)


TURN = (2, 0, 1)
KEPT = 80
UNIQUE = 16 * KEPT


def runs(start, count, *stops):
    out = []
    while count:
        start %= O
        n = min([count, O - start] + [p - start for p in stops if p > start])
        out.append((start, n))
        start, count = start + n, count - n
    return out


def pair_sum_kernel(a_any, hi_ref, lo_ref, a_ref, rest, sem):
    read = pltpu.make_async_copy(a_any, a_ref, sem)
    read.start()
    read.wait()

    @pl.loop(0, PAIRS // THIRD, unroll=8)
    def _(g):
        both = a_ref[pl.ds(pl.multiple_of(g * SLAB + 4 * THIRD, 8), 8), :]
        rest[pl.ds(pl.multiple_of(g * THIRD, 8), 8), :] = both
        rest[pl.ds(pl.multiple_of(g * THIRD + 8, 8), 8), :] = pltpu.roll(both, 64, 1)
        last = a_ref[pl.ds(pl.multiple_of(g * SLAB + 4 * THIRD + 8, 8), 8), :]
        rest[pl.ds(pl.multiple_of(g * THIRD + 16, 8), 8), :] = last

    def straight(t, i, j, n):
        if t == 4:
            return rest[i * O + j : i * O + j + n, :]
        at = (2 * i + j // THIRD) * SLAB + t * THIRD + j % THIRD
        return a_ref[at : at + n, :]

    def mirrored(t, i, j, n):
        if t == 4:
            return rest[pl.ds(j * O + i, n, stride=O), :]
        return a_ref[pl.ds((2 * j + i // THIRD) * SLAB + t * THIRD + i % THIRD, n, stride=2 * SLAB), :]

    for t in range(5):
        for q in range(16):
            rows = []
            for k in range(3):
                i, m = 3 * q + TURN[k], int(k == 0)
                rows += [
                    straight(t, i, j, n) + mirrored(t, i, j, n) for j, n in runs(3 * q + m, 27 - m, THIRD)
                ]
            s = jnp.concatenate(rows, axis=0)
            if t == 4:
                s = jnp.where(lax.broadcasted_iota(jnp.int32, s.shape, 1) < 64, s, 0)
            at, lanes = slice(q * KEPT, (q + 1) * KEPT), slice(t * 128, (t + 1) * 128)
            hi_ref[at, lanes], lo_ref[at, lanes] = split(s)


def pair_sum(a):
    return pl.pallas_call(
        pair_sum_kernel,
        out_shape=[jax.ShapeDtypeStruct((UNIQUE, WIDE), BF16)] * 2,
        in_specs=[pl.BlockSpec(memory_space=pl.ANY)],
        out_specs=[pl.BlockSpec(memory_space=pltpu.VMEM)] * 2,
        scratch_shapes=[
            pltpu.VMEM((32 * 3 * SLAB, 128), F32),
            pltpu.VMEM((PAIRS, 128), F32),
            pltpu.SemaphoreType.DMA,
        ],
        compiler_params=pltpu.CompilerParams(vmem_limit_bytes=24 << 20),
    )(a)


def ladder_kernel(
    hi_ref, lo_ref, b_ref, o_ref, b_hi, b_lo, away, acc, other, r1, s1, r2, s2, r3, mine, r4, ends, r5, ssem, rsem
):
    v = lax.axis_index("vir")
    core, zh = lax.rem(v, 2), v // 2
    me = occ_place()
    r = lax.axis_index("occ")
    q, zl = r // 2, me["z"]
    barrier = pltpu.get_barrier_semaphore()

    def triple(k):
        return (lax.rem(q + k, 16) * 2 + zl, v)

    def high(k):
        to = lax.rem(zh + k, 4)
        return to, (r, to * 2 + core)

    twin = (r, v + 1 - 2 * core)
    beside = (r + 1 - 2 * zl, v)
    devices = [twin, beside] + [triple(k) for k in range(1, 16)] + [high(k)[1] for k in range(1, 4)]
    for d in devices:
        pl.semaphore_signal(barrier, inc=1, device_id=d, device_id_type=MESH)

    sent = [0]

    def remote(src, dst, device):
        n = sent[0]
        sent[0] += 1
        c = pltpu.make_async_remote_copy(
            src_ref=src, dst_ref=dst, send_sem=ssem.at[n], recv_sem=rsem.at[n], device_id=device, device_id_type=MESH
        )
        c.start()
        return c

    @pl.loop(0, DEPTH // 48)
    def _(k):
        rows = pl.ds(pl.multiple_of(k * 48, 16), 48)
        b = b_ref[rows, :]
        for c in range(2):
            for h in range(2):
                at = [(2 * h + e) * 384 + c * 192 for e in range(2)]
                piece = jnp.concatenate([b[:, p : p + 192] for p in at], axis=1)
                b_hi[c * 2 + h, rows, :], b_lo[c * 2 + h, rows, :] = split(piece)

    def product(n, out, h):
        @pl.loop(0, UNIQUE // 256)
        def _(m):
            rows = pl.ds(pl.multiple_of(m * 256, 256), 256)
            dot = functools.partial(jnp.dot, preferred_element_type=F32)
            hi, lo = hi_ref[rows, :DEPTH], lo_ref[rows, :DEPTH]
            out[h, rows, :] = dot(hi, b_lo[n]) + dot(lo, b_hi[n]) + dot(hi, b_hi[n])

    swap = []
    for h in range(2):
        product((1 - core) * 2 + h, away, h)
        if h == 0:
            pl.semaphore_wait(barrier, len(devices))
        swap.append(remote(away.at[h], other.at[h], twin))

    first = [[], []]
    for h in range(2):
        product(core * 2 + h, acc, h)
        swap[h].wait()

        @pl.loop(0, 16)
        def _(m):
            rows = pl.ds(pl.multiple_of(m * KEPT, 8), KEPT)
            acc[h, rows, :] += other[h, rows, :]

        dim = "yx"[h]
        for k in range(1, 4):
            at, rank = occ_peer(me, dim, k)
            if h == 0:
                rows = pl.ds(pl.multiple_of(at * 4 * KEPT, 8), 4 * KEPT)
                first[h].append(remote(acc.at[h, rows], r1.at[h, k - 1], (rank, v)))
            else:
                for y in range(4):
                    rows = pl.ds(pl.multiple_of((y * 4 + at) * KEPT, 8), KEPT)
                    first[h].append(remote(acc.at[h, rows], r1.at[h, k - 1, pl.ds(y * KEPT, KEPT)], (rank, v)))

    second = [[], []]
    for h in range(2):
        for c in first[h]:
            c.wait()
        for y in range(4):
            part = pl.ds(y * KEPT, KEPT)
            base = (me["y"] * 4 + y) if h == 0 else (y * 4 + me["x"])
            own = pl.ds(pl.multiple_of(base * KEPT, 8), KEPT)
            s1[h, part, :] = (acc[h, own, :] + r1[h, 0, part, :]) + (r1[h, 1, part, :] + r1[h, 2, part, :])
        for k in range(1, 4):
            at, rank = occ_peer(me, "xy"[h], k)
            rows = pl.ds(pl.multiple_of(at * KEPT, 8), KEPT)
            second[h].append(remote(s1.at[h, rows], r2.at[h, k - 1], (rank, v)))

    for h in range(2):
        for c in second[h]:
            c.wait()
        own = pl.ds(pl.multiple_of(me["xy"[h]] * KEPT, 8), KEPT)
        s2[h] = (s1[h, own, :] + r2[h, 0]) + (r2[h, 1] + r2[h, 2])

    def part(to):
        return s2.at[to // 2, :, pl.ds(pl.multiple_of(lax.rem(to, 2) * 128, 128), 256)]

    third = [remote(part(high(k)[0]), r3.at[k - 1], high(k)[1]) for k in range(1, 4)]
    total = part(zh)[...]
    for k in range(1, 4):
        third[k - 1].wait()
        total += r3[k - 1]
    mine[...] = jnp.where(lax.rem(zh, 2) == 0, total[:, :192], total[:, 64:])
    fourth = remote(mine, r4, beside)
    fourth.wait()
    u = mine[...] + r4[...]

    def kept(k, m):
        return u[27 * k - 1 + m : 27 * k + m]

    fifth = []
    for k in range(1, 8):
        ends[k - 1, :9] = jnp.concatenate([kept(e, 3 * k + t) for t in range(3) for e in (1, 2, 0)], axis=0)
        fifth.append(remote(ends.at[k - 1], r5.at[k - 1], triple(k)))
    for c in fifth:
        c.wait()
    turned = []
    for t in range(3):
        k = TURN.index(t)
        rows = [u[27 * k - 1 : 27 * k + 26]] if k else [kept(1, 2), u[0:26]]
        rows += [r5[6 - e, 3 * t : 3 * t + 3] for e in range(7)]
        turned.append(pltpu.roll(jnp.concatenate(rows, axis=0), 3 * q, 0))
    low = jnp.concatenate([turned[0], turned[1][:24]], axis=0)
    top = jnp.concatenate([turned[1][24:], turned[2]], axis=0)
    o_ref[...] = jnp.where(zl == 0, low, top)


def ladder(hi, lo, b):
    return pl.pallas_call(
        ladder_kernel,
        out_shape=jax.ShapeDtypeStruct((ROWS, 192), F32),
        in_specs=[pl.BlockSpec(memory_space=pltpu.VMEM)] * 3,
        out_specs=pl.BlockSpec(memory_space=pltpu.VMEM),
        scratch_shapes=[
            pltpu.VMEM((4, DEPTH, 384), BF16),
            pltpu.VMEM((4, DEPTH, 384), BF16),
            pltpu.VMEM((2, UNIQUE, 384), F32),
            pltpu.VMEM((2, UNIQUE, 384), F32),
            pltpu.VMEM((2, UNIQUE, 384), F32),
            pltpu.VMEM((2, 3, 4 * KEPT, 384), F32),
            pltpu.VMEM((2, 4 * KEPT, 384), F32),
            pltpu.VMEM((2, 3, KEPT, 384), F32),
            pltpu.VMEM((2, KEPT, 384), F32),
            pltpu.VMEM((3, KEPT, 256), F32),
            pltpu.VMEM((KEPT, 192), F32),
            pltpu.VMEM((KEPT, 192), F32),
            pltpu.VMEM((7, 16, 192), F32),
            pltpu.VMEM((7, 16, 192), F32),
            pltpu.SemaphoreType.DMA((34,)),
            pltpu.SemaphoreType.DMA((34,)),
        ],
        compiler_params=pltpu.CompilerParams(collective_id=1, has_side_effects=True, vmem_limit_bytes=48 << 20),
    )(hi, lo, b)


def on_device(amplitudes, integrals):
    columns = exchange(amplitudes).reshape(32 * 3 * SLAB, 128)
    slab_matrix = integrals.transpose(1, 0, 2).reshape(DEPTH, COLS)
    return ladder(*pair_sum(columns), slab_matrix)


def solution(mesh):
    in_specs = (P("occ", "vir", None), P("vir", "occ", None))
    out_specs = P("occ", "vir")
    return jax.shard_map(
        on_device, mesh=mesh, in_specs=in_specs, out_specs=out_specs, check_vma=False
    )
```

```python
import functools

import jax
import jax.numpy as jnp
from jax import lax
from jax.experimental import pallas as pl
from jax.experimental.pallas import tpu as pltpu
from jax.sharding import PartitionSpec as P

O = 48
MESH = pl.DeviceIdType.MESH
F32, BF16 = jnp.float32, jnp.bfloat16
SIZE = {"y": 4, "x": 4, "z": 2}
AXIS = {"y": 0, "x": 1, "z": 2}
ORDERS = (("y", "x", "z"), ("x", "z", "y"), ("z", "y", "x"))
ROWS, DEPTH, WIDE, COLS = 72, 576, 640, 1536
PAIRS = 2304


def occ_place():
    r = lax.axis_index("occ")
    return {"y": r // 8, "x": lax.rem(r // 2, 4), "z": lax.rem(r, 2)}


def occ_peer(me, dim, k):
    c = dict(me)
    c[dim] = lax.rem(me[dim] + k, SIZE[dim])
    return c[dim], c["y"] * 8 + c["x"] * 2 + c["z"]


THIRD = ROWS // 3
BLOCK_AT = (0, 32, 72, 112)
SLAB = BLOCK_AT[3]
PITCH = 392

TURN = (2, 0, 1)
KEPT = 80
UNIQUE = 16 * KEPT


def split(x):
    hi = x.astype(BF16)
    return hi, (x - hi.astype(F32)).astype(BF16)


def ladder_kernel(
    x_ref, b_any, o_ref,
    x, b_ref, turned, g0, g1, g2, g3, rest, s_hi, s_lo, b_hi, b_lo,
    away, other, acc, r1, s1, r2, s2, r3, mine, r4, ends, r5,
    ssem, rsem, lsem, xsem,
):
    v = lax.axis_index("vir")
    r = lax.axis_index("occ")
    core, zh = lax.rem(v, 2), v // 2
    me = occ_place()
    q, zl = r // 2, me["z"]
    reads = [pltpu.make_async_copy(x_ref.at[pl.ds(t * THIRD, THIRD)], x.at[t], xsem.at[t]) for t in range(3)]
    reads.append(pltpu.make_async_copy(b_any, b_ref, xsem.at[3]))
    for c in reads:
        c.start()

    def triple(k):
        return (lax.rem(q + k, 16) * 2 + zl, v)

    def high(k):
        to = lax.rem(zh + k, 4)
        return to, (r, to * 2 + core)

    twin = (r, v + 1 - 2 * core)
    beside = (r + 1 - 2 * zl, v)
    devices = [twin, beside] + [triple(k) for k in range(1, 16)] + [high(k)[1] for k in range(1, 4)]
    barrier = pltpu.get_barrier_semaphore()
    for d in devices:
        pl.semaphore_signal(barrier, inc=1, device_id=d, device_id_type=MESH)

    sent = [0, 0]

    def remote(src, dst, device):
        n = sent[0]
        sent[0] += 1
        c = pltpu.make_async_remote_copy(
            src_ref=src, dst_ref=dst, send_sem=ssem.at[n], recv_sem=rsem.at[n], device_id=device, device_id_type=MESH
        )
        c.start()
        return c

    lane = lax.broadcasted_iota(jnp.int32, (8, 128), 1)

    def regroup(t, block):
        @pl.loop(0, 8, unroll=8)
        def _(p):
            turned[pl.ds(pl.multiple_of(p * PITCH, 8), 384), 0:O] = x[t, block * 8 + p].T

        @pl.loop(0, 32, unroll=8)
        def _(to):
            at = (t, to // 8, lax.rem(to // 2, 4), lax.rem(to, 2))
            tiles = [jnp.zeros((8, 128), F32)] * 5
            for d in range(12):
                tile, off = d * O // 128, d * O % 128
                piece = turned[pl.ds(to * 12 + d, 8, stride=PITCH), :]
                if off:
                    piece = pltpu.roll(piece, off, 1)
                tiles[tile] = jnp.where((lane >= off) & (lane < off + O), piece, tiles[tile])
                if off + O > 128:
                    tiles[tile + 1] = jnp.where(lane < off + O - 128, piece, tiles[tile + 1])
            for n in range(4):
                g0[(*at, slice(BLOCK_AT[block] + 8 * n, BLOCK_AT[block] + 8 * n + 8))] = tiles[n]
            behind = (*at, slice(64, 72) if block < 2 else slice(104, 112))
            if block == 1:
                g0[behind] = jnp.where(lane < 64, g0[behind], pltpu.roll(tiles[4], 64, 1))
            else:
                g0[behind] = tiles[4]

    def view(ref, t, dim, at, rows):
        ix = [slice(None)] * 3
        ix[AXIS[dim]] = at
        if ref is g3:
            return ref.at[ix[0], ix[1], ix[2], t, rows]
        return ref.at[t, ix[0], ix[1], ix[2], rows]

    held = [g0, g1, g2, g3]

    def start(t, s, rows):
        dim = ORDERS[t][s]
        src, dst = held[s], held[s + 1]
        copies = []
        for k in range(1, SIZE[dim]):
            at, rank = occ_peer(me, dim, k)
            copies.append(remote(view(src, t, dim, at, rows), view(dst, t, dim, me[dim], rows), (rank, v)))
        own = pltpu.make_async_copy(
            view(src, t, dim, me[dim], rows), view(dst, t, dim, me[dim], rows), lsem.at[sent[1]]
        )
        sent[1] += 1
        own.start()
        return copies + [own]

    flying = [[], [], []]
    for block in range(3):
        rows = pl.ds(BLOCK_AT[block], BLOCK_AT[block + 1] - BLOCK_AT[block])
        for t in range(3):
            if block == 0:
                reads[t].wait()
            regroup(t, block)
            if block == t == 0:
                pl.semaphore_wait(barrier, len(devices))
            flying[t] += start(t, 0, rows)

    reads[3].wait()

    @pl.loop(0, DEPTH // 48)
    def _(k):
        rows = pl.ds(pl.multiple_of(k * 48, 16), 48)
        b = b_ref[rows, :]
        for c in range(2):
            piece = jnp.concatenate([b[:, e * 384 + c * 192 : e * 384 + c * 192 + 192] for e in range(4)], axis=1)
            for n in range(3):
                b_hi[c * 3 + n, rows, :], b_lo[c * 3 + n, rows, :] = split(piece[:, n * 256 : (n + 1) * 256])

    for s in (1, 2, 3):
        following = []
        for t in range(3):
            for c in flying[t]:
                c.wait()
            if s < 3:
                following.append(start(t, s, pl.ds(0, SLAB)))
        flying = following

    flat = g3.reshape(32 * 3 * SLAB, 128)

    @pl.loop(0, PAIRS // THIRD, unroll=8)
    def _(g):
        both = flat[pl.ds(pl.multiple_of(g * SLAB + 64, 8), 8), :]
        rest[pl.ds(pl.multiple_of(g * THIRD, 8), 8), :] = both
        rest[pl.ds(pl.multiple_of(g * THIRD + 8, 8), 8), :] = pltpu.roll(both, 64, 1)
        rest[pl.ds(pl.multiple_of(g * THIRD + 16, 8), 8), :] = flat[pl.ds(pl.multiple_of(g * SLAB + 104, 8), 8), :]

    def place(t, p):
        return p // THIRD * SLAB + BLOCK_AT[p % THIRD // 8] + t * 8 + p % 8

    def straight(t, i, j, n):
        tiles = []
        for block in range(j // 8, (j + n + 7) // 8):
            p = i * O + block % 6 * 8
            tiles.append(rest[p : p + 8, :] if t == 4 else flat[pl.ds(place(t, p), 8), :])
        return jnp.concatenate(tiles, axis=0)[j % 8 : j % 8 + n]

    def mirrored(t, i, j, n):
        parts = []
        for first, count in ((j, min(n, O - j)), (0, n - min(n, O - j))):
            if count and t == 4:
                parts.append(rest[pl.ds(first * O + i, count, stride=O), :])
            elif count:
                parts.append(flat[pl.ds(place(t, first * O + i), count, stride=2 * SLAB), :])
        return jnp.concatenate(parts, axis=0)

    for t in range(5):
        for own in range(16):
            sums = []
            for k in range(3):
                i, m = 3 * own + TURN[k], int(k == 0)
                sums.append(straight(t, i, 3 * own + m, 27 - m) + mirrored(t, i, 3 * own + m, 27 - m))
            total = jnp.concatenate(sums, axis=0)
            if t == 4:
                total = jnp.where(lax.broadcasted_iota(jnp.int32, total.shape, 1) < 64, total, 0)
            at, lanes = slice(own * KEPT, (own + 1) * KEPT), slice(t * 128, (t + 1) * 128)
            s_hi[at, lanes], s_lo[at, lanes] = split(total)


    def product(n):
        @pl.loop(0, UNIQUE // 256)
        def _(m):
            rows = pl.ds(pl.multiple_of(m * 256, 256), 256)
            dot = functools.partial(jnp.dot, preferred_element_type=F32)

            def multiply(at):
                hi, lo = s_hi[rows, :DEPTH], s_lo[rows, :DEPTH]
                return dot(hi, b_lo[at]) + dot(lo, b_hi[at]) + dot(hi, b_hi[at])

            if n >= 3:
                away[n - 3, rows, :] = multiply((1 - core) * 3 + n - 3)
            else:
                both = multiply(core * 3 + n)
                acc[2 * n, rows, :] = both[:, :128]
                acc[2 * n + 1, rows, :] = both[:, 128:]

    swap, first, second = [], [], []
    for n in (3, 4, 0, 5, 1, 2):
        product(n)
        if n >= 3:
            swap.append(remote(away.at[n - 3], other.at[n - 3], twin))
            continue
        swap[n].wait()

        @pl.loop(0, 16)
        def _(m):
            rows = pl.ds(pl.multiple_of(m * KEPT, 8), KEPT)
            acc[2 * n, rows, :] += other[n, rows, :128]
            acc[2 * n + 1, rows, :] += other[n, rows, 128:]

        copies = []
        for k in range(1, 4):
            at, rank = occ_peer(me, "y", k)
            rows = pl.ds(pl.multiple_of(at * 4 * KEPT, 8), 4 * KEPT)
            copies.append(remote(acc.at[2 * n, rows], r1.at[2 * n, k - 1], (rank, v)))
            at, rank = occ_peer(me, "x", k)
            for y in range(4):
                rows = pl.ds(pl.multiple_of((y * 4 + at) * KEPT, 8), KEPT)
                to = r1.at[2 * n + 1, k - 1, pl.ds(y * KEPT, KEPT)]
                copies.append(remote(acc.at[2 * n + 1, rows], to, (rank, v)))
        first.append(copies)

    for n in range(3):
        for c in first[n]:
            c.wait()
        copies = []
        for h in range(2):
            e = 2 * n + h
            for y in range(4):
                part = pl.ds(y * KEPT, KEPT)
                base = (me["y"] * 4 + y) if h == 0 else (y * 4 + me["x"])
                own = pl.ds(pl.multiple_of(base * KEPT, 8), KEPT)
                s1[e, part, :] = (acc[e, own, :] + r1[e, 0, part, :]) + (r1[e, 1, part, :] + r1[e, 2, part, :])
            for k in range(1, 4):
                at, rank = occ_peer(me, "xy"[h], k)
                rows = pl.ds(pl.multiple_of(at * KEPT, 8), KEPT)
                copies.append(remote(s1.at[e, rows], r2.at[e, k - 1], (rank, v)))
        second.append(copies)

    for n in range(3):
        for c in second[n]:
            c.wait()
        for h in range(2):
            e = 2 * n + h
            own = pl.ds(pl.multiple_of(me["xy"[h]] * KEPT, 8), KEPT)
            s2[e] = (s1[e, own, :] + r2[e, 0]) + (r2[e, 1] + r2[e, 2])

    def part(to):
        return s2.at[pl.ds(to // 2 * 3 + lax.rem(to, 2), 2)]

    third = [remote(part(high(k)[0]), r3.at[k - 1], high(k)[1]) for k in range(1, 4)]
    total = part(zh)[...]
    for k in range(1, 4):
        third[k - 1].wait()
        total += r3[k - 1]
    total = jnp.concatenate([total[0], total[1]], axis=1)
    mine[...] = jnp.where(lax.rem(zh, 2) == 0, total[:, :192], total[:, 64:])
    fourth = remote(mine, r4, beside)
    fourth.wait()
    u = mine[...] + r4[...]

    def kept(k, m):
        return u[27 * k - 1 + m : 27 * k + m]

    fifth = []
    for k in range(1, 8):
        ends[k - 1, :9] = jnp.concatenate([kept(e, 3 * k + t) for t in range(3) for e in (1, 2, 0)], axis=0)
        fifth.append(remote(ends.at[k - 1], r5.at[k - 1], triple(k)))
    for c in fifth:
        c.wait()
    turned = []
    for t in range(3):
        k = TURN.index(t)
        rows = [u[27 * k - 1 : 27 * k + 26]] if k else [kept(1, 2), u[0:26]]
        rows += [r5[6 - e, 3 * t : 3 * t + 3] for e in range(7)]
        turned.append(pltpu.roll(jnp.concatenate(rows, axis=0), 3 * q, 0))
    low = jnp.concatenate([turned[0], turned[1][:24]], axis=0)
    top = jnp.concatenate([turned[1][24:], turned[2]], axis=0)
    o_ref[...] = jnp.where(zl == 0, low, top)


def ladder(x, b):
    slabs = pltpu.VMEM((3, 4, 4, 2, SLAB, 128), F32)
    return pl.pallas_call(
        ladder_kernel,
        out_shape=jax.ShapeDtypeStruct((ROWS, 192), F32),
        in_specs=[pl.BlockSpec(memory_space=pl.ANY)] * 2,
        out_specs=pl.BlockSpec(memory_space=pltpu.VMEM),
        scratch_shapes=[
            pltpu.VMEM((3, THIRD, O, 384), F32),
            pltpu.VMEM((DEPTH, COLS), F32),
            pltpu.VMEM((8 * PITCH, 128), F32),
            slabs,
            slabs,
            slabs,
            pltpu.VMEM((4, 4, 2, 3, SLAB, 128), F32),
            pltpu.VMEM((PAIRS, 128), F32),
            pltpu.VMEM((UNIQUE, WIDE), BF16),
            pltpu.VMEM((UNIQUE, WIDE), BF16),
            pltpu.VMEM((6, DEPTH, 256), BF16),
            pltpu.VMEM((6, DEPTH, 256), BF16),
            pltpu.VMEM((3, UNIQUE, 256), F32),
            pltpu.VMEM((3, UNIQUE, 256), F32),
            pltpu.VMEM((6, UNIQUE, 128), F32),
            pltpu.VMEM((6, 3, 4 * KEPT, 128), F32),
            pltpu.VMEM((6, 4 * KEPT, 128), F32),
            pltpu.VMEM((6, 3, KEPT, 128), F32),
            pltpu.VMEM((6, KEPT, 128), F32),
            pltpu.VMEM((3, 2, KEPT, 128), F32),
            pltpu.VMEM((KEPT, 192), F32),
            pltpu.VMEM((KEPT, 192), F32),
            pltpu.VMEM((7, 16, 192), F32),
            pltpu.VMEM((7, 16, 192), F32),
            pltpu.SemaphoreType.DMA((112,)),
            pltpu.SemaphoreType.DMA((112,)),
            pltpu.SemaphoreType.DMA((15,)),
            pltpu.SemaphoreType.DMA((4,)),
        ],
        compiler_params=pltpu.CompilerParams(collective_id=0, has_side_effects=True, vmem_limit_bytes=62 << 20),
    )(x, b)


def on_device(amplitudes, integrals):
    slab_matrix = integrals.transpose(1, 0, 2).reshape(DEPTH, COLS)
    return ladder(amplitudes, slab_matrix)


def solution(mesh):
    in_specs = (P("occ", "vir", None), P("vir", "occ", None))
    out_specs = P("occ", "vir")
    return jax.shard_map(
        on_device, mesh=mesh, in_specs=in_specs, out_specs=out_specs, check_vma=False
    )
```

```python
import functools

import jax
import jax.numpy as jnp
from jax import lax
from jax.experimental import pallas as pl
from jax.experimental.pallas import tpu as pltpu
from jax.sharding import PartitionSpec as P

O = 48
MESH = pl.DeviceIdType.MESH
F32, BF16 = jnp.float32, jnp.bfloat16
SIZE = {"y": 4, "x": 4, "z": 2}
AXIS = {"y": 0, "x": 1, "z": 2}
ORDERS = (("y", "x", "z"), ("x", "z", "y"), ("z", "y", "x"))
ROWS, DEPTH, WIDE, COLS = 72, 576, 640, 1536
PAIRS = 2304


def occ_place():
    r = lax.axis_index("occ")
    return {"y": r // 8, "x": lax.rem(r // 2, 4), "z": lax.rem(r, 2)}


def occ_peer(me, dim, k):
    c = dict(me)
    c[dim] = lax.rem(me[dim] + k, SIZE[dim])
    return c[dim], c["y"] * 8 + c["x"] * 2 + c["z"]


THIRD = ROWS // 3
BLOCK_AT = (0, 32, 72, 112)
SLAB = BLOCK_AT[3]
PITCH = 392

TURN = (2, 0, 1)
KEPT = 80
UNIQUE = 16 * KEPT
CHUNK = 640


def split(x):
    hi = x.astype(BF16)
    return hi, (x - hi.astype(F32)).astype(BF16)


def ladder_kernel(
    x_ref, b_any, o_ref,
    x, b_ref, turned, g0, g1, g2, g3, rest, s_hi, s_lo, b_hi, b_lo,
    away, other, acc, r1, s1, r2, s2, r3, mine, r4, ends, r5,
    ssem, rsem, lsem, xsem, zsem,
):
    v = lax.axis_index("vir")
    r = lax.axis_index("occ")
    core, zh = lax.rem(v, 2), v // 2
    me = occ_place()
    q, zl = r // 2, me["z"]
    reads = [pltpu.make_async_copy(x_ref.at[pl.ds(t * THIRD, THIRD)], x.at[t], xsem.at[t]) for t in range(3)]
    reads.append(pltpu.make_async_copy(b_any, b_ref, xsem.at[3]))
    for c in reads:
        c.start()

    def triple(k):
        return (lax.rem(q + k, 16) * 2 + zl, v)

    twin = (r, v + 1 - 2 * core)
    beside = (r + 1 - 2 * zl, v)
    devices = [twin, beside] + [triple(k) for k in range(1, 16)] + [(r, lax.rem(zh + k, 4) * 2 + core) for k in range(1, 4)]
    barrier = pltpu.get_barrier_semaphore()
    for d in devices:
        pl.semaphore_signal(barrier, inc=1, device_id=d, device_id_type=MESH)

    sent = [0, 0]

    def remote(src, dst, device):
        n = sent[0]
        sent[0] += 1
        c = pltpu.make_async_remote_copy(
            src_ref=src, dst_ref=dst, send_sem=ssem.at[n], recv_sem=rsem.at[n], device_id=device, device_id_type=MESH
        )
        c.start()
        return c

    lane = lax.broadcasted_iota(jnp.int32, (8, 128), 1)

    def regroup(t, block):
        @pl.loop(0, 8, unroll=8)
        def _(p):
            turned[pl.ds(pl.multiple_of(p * PITCH, 8), 384), 0:O] = x[t, block * 8 + p].T

        @pl.loop(0, 32, unroll=8)
        def _(to):
            at = (t, to // 8, lax.rem(to // 2, 4), lax.rem(to, 2))
            tiles = [jnp.zeros((8, 128), F32)] * 5
            for d in range(12):
                tile, off = d * O // 128, d * O % 128
                piece = turned[pl.ds(to * 12 + d, 8, stride=PITCH), :]
                if off:
                    piece = pltpu.roll(piece, off, 1)
                tiles[tile] = jnp.where((lane >= off) & (lane < off + O), piece, tiles[tile])
                if off + O > 128:
                    tiles[tile + 1] = jnp.where(lane < off + O - 128, piece, tiles[tile + 1])
            for n in range(4):
                g0[(*at, slice(BLOCK_AT[block] + 8 * n, BLOCK_AT[block] + 8 * n + 8))] = tiles[n]
            behind = (*at, slice(64, 72) if block < 2 else slice(104, 112))
            if block == 1:
                g0[behind] = jnp.where(lane < 64, g0[behind], pltpu.roll(tiles[4], 64, 1))
            else:
                g0[behind] = tiles[4]

    def view(ref, t, dim, at, rows):
        ix = [slice(None)] * 3
        ix[AXIS[dim]] = at
        if ref is g3:
            return ref.at[ix[0], ix[1], ix[2], t, rows]
        return ref.at[t, ix[0], ix[1], ix[2], rows]

    held = [g0, g1, g2, g3]

    def start(t, s, block):
        dim = ORDERS[t][s]
        rows = pl.ds(BLOCK_AT[block], BLOCK_AT[block + 1] - BLOCK_AT[block])
        src, dst = held[s], held[s + 1]
        copies = []
        for k in range(1, SIZE[dim]):
            at, rank = occ_peer(me, dim, k)
            copies.append(remote(view(src, t, dim, at, rows), view(dst, t, dim, me[dim], rows), (rank, v)))
        own = pltpu.make_async_copy(
            view(src, t, dim, me[dim], rows), view(dst, t, dim, me[dim], rows), lsem.at[sent[1]]
        )
        sent[1] += 1
        own.start()
        return copies + [own]

    flying = {}
    for block in range(3):
        for t in range(3):
            if block == 0:
                reads[t].wait()
            regroup(t, block)
            if block == t == 0:
                pl.semaphore_wait(barrier, len(devices))
            flying[t, block] = start(t, 0, block)

    def onward(s):
        for block in range(3):
            for t in range(3):
                for c in flying[t, block]:
                    c.wait()
                if s < 3:
                    flying[t, block] = start(t, s, block)

    onward(1)

    reads[3].wait()

    @pl.loop(0, DEPTH // 48)
    def _(k):
        rows = pl.ds(pl.multiple_of(k * 48, 16), 48)
        b = b_ref[rows, :]
        for c in range(2):
            piece = jnp.concatenate([b[:, e * 384 + c * 192 : e * 384 + c * 192 + 192] for e in range(4)], axis=1)
            for n in range(3):
                b_hi[c * 3 + n, rows, :], b_lo[c * 3 + n, rows, :] = split(piece[:, n * 256 : (n + 1) * 256])

    onward(2)
    onward(3)

    flat = g3.reshape(32 * 3 * SLAB, 128)

    @pl.loop(0, PAIRS // THIRD, unroll=8)
    def _(g):
        both = flat[pl.ds(pl.multiple_of(g * SLAB + 64, 8), 8), :]
        rest[pl.ds(pl.multiple_of(g * THIRD, 8), 8), :] = both
        rest[pl.ds(pl.multiple_of(g * THIRD + 8, 8), 8), :] = pltpu.roll(both, 64, 1)
        rest[pl.ds(pl.multiple_of(g * THIRD + 16, 8), 8), :] = flat[pl.ds(pl.multiple_of(g * SLAB + 104, 8), 8), :]

    def place(t, p):
        return p // THIRD * SLAB + BLOCK_AT[p % THIRD // 8] + t * 8 + p % 8

    def straight(t, i, j, n):
        tiles = []
        for block in range(j // 8, (j + n + 7) // 8):
            p = i * O + block % 6 * 8
            tiles.append(rest[p : p + 8, :] if t == 4 else flat[pl.ds(place(t, p), 8), :])
        return jnp.concatenate(tiles, axis=0)[j % 8 : j % 8 + n]

    def mirrored(t, i, j, n):
        parts = []
        for first, count in ((j, min(n, O - j)), (0, n - min(n, O - j))):
            if count and t == 4:
                parts.append(rest[pl.ds(first * O + i, count, stride=O), :])
            elif count:
                parts.append(flat[pl.ds(place(t, first * O + i), count, stride=2 * SLAB), :])
        return jnp.concatenate(parts, axis=0)

    for t in range(5):
        for own in range(16):
            sums = []
            for k in range(3):
                i, m = 3 * own + TURN[k], int(k == 0)
                sums.append(straight(t, i, 3 * own + m, 27 - m) + mirrored(t, i, 3 * own + m, 27 - m))
            total = jnp.concatenate(sums, axis=0)
            if t == 4:
                total = jnp.where(lax.broadcasted_iota(jnp.int32, total.shape, 1) < 64, total, 0)
            at, lanes = slice(own * KEPT, (own + 1) * KEPT), slice(t * 128, (t + 1) * 128)
            s_hi[at, lanes], s_lo[at, lanes] = split(total)


    def product(n):
        @pl.loop(0, UNIQUE // CHUNK)
        def _(m):
            rows = pl.ds(pl.multiple_of(m * CHUNK, 128), CHUNK)
            dot = functools.partial(jnp.dot, preferred_element_type=F32)

            def multiply(at):
                hi, lo = s_hi[rows, :DEPTH], s_lo[rows, :DEPTH]
                return dot(hi, b_lo[at]) + dot(lo, b_hi[at]) + dot(hi, b_hi[at])

            if n >= 3:
                away[n - 3, rows, :] = multiply((1 - core) * 3 + n - 3)
            else:
                both = multiply(core * 3 + n)
                acc[2 * n, rows, :] = both[:, :128]
                acc[2 * n + 1, rows, :] = both[:, 128:]

    swap, first, second = [], [], []
    for n in (3, 4, 0, 5, 1, 2):
        product(n)
        if n >= 3:
            swap.append(remote(away.at[n - 3], other.at[n - 3], twin))
            continue
        swap[n].wait()

        @pl.loop(0, 16)
        def _(m):
            rows = pl.ds(pl.multiple_of(m * KEPT, 8), KEPT)
            acc[2 * n, rows, :] += other[n, rows, :128]
            acc[2 * n + 1, rows, :] += other[n, rows, 128:]

        copies = []
        for k in range(1, 4):
            at, rank = occ_peer(me, "y", k)
            rows = pl.ds(pl.multiple_of(at * 4 * KEPT, 8), 4 * KEPT)
            copies.append(remote(acc.at[2 * n, rows], r1.at[2 * n, k - 1], (rank, v)))
            at, rank = occ_peer(me, "x", k)
            for y in range(4):
                rows = pl.ds(pl.multiple_of((y * 4 + at) * KEPT, 8), KEPT)
                to = r1.at[2 * n + 1, k - 1, pl.ds(y * KEPT, KEPT)]
                copies.append(remote(acc.at[2 * n + 1, rows], to, (rank, v)))
        first.append(copies)

    for n in range(3):
        for c in first[n]:
            c.wait()
        copies = []
        for h in range(2):
            e = 2 * n + h
            for y in range(4):
                part = pl.ds(y * KEPT, KEPT)
                base = (me["y"] * 4 + y) if h == 0 else (y * 4 + me["x"])
                own = pl.ds(pl.multiple_of(base * KEPT, 8), KEPT)
                s1[e, part, :] = (acc[e, own, :] + r1[e, 0, part, :]) + (r1[e, 1, part, :] + r1[e, 2, part, :])
            for k in range(1, 4):
                at, rank = occ_peer(me, "xy"[h], k)
                rows = pl.ds(pl.multiple_of(at * KEPT, 8), KEPT)
                copies.append(remote(s1.at[e, rows], r2.at[e, k - 1], (rank, v)))
        second.append(copies)

    third = []
    for n in range(3):
        for c in second[n]:
            c.wait()
        for h in range(2):
            e = 2 * n + h
            own = pl.ds(pl.multiple_of(me["xy"[h]] * KEPT, 8), KEPT)
            s2[e] = (s1[e, own, :] + r2[e, 0]) + (r2[e, 1] + r2[e, 2])
            for half in range(2):
                if e % 3 == 2 - 2 * half:
                    continue
                to = e // 3 * 2 + half
                slot, k = e % 3 - half, lax.rem(zh - to + 4, 4)
                c = pltpu.make_async_remote_copy(
                    src_ref=s2.at[e],
                    dst_ref=r3.at[slot, lax.max(k - 1, 0)],
                    send_sem=ssem.at[sent[0]],
                    recv_sem=zsem.at[slot, lax.max(k - 1, 0)],
                    device_id=(r, to * 2 + core),
                    device_id_type=MESH,
                )
                sent[0] += 1
                third.append((to, c))
                pl.when(zh != to)(c.start)
    for to, c in third:
        pl.when(zh != to)(c.wait_send)
    total = s2[pl.ds(zh // 2 * 3 + lax.rem(zh, 2), 2)]
    for k in range(3):
        for slot in range(2):
            pltpu.make_async_remote_copy(
                src_ref=s2.at[slot], dst_ref=r3.at[slot, k], send_sem=ssem.at[0], recv_sem=zsem.at[slot, k],
                device_id=twin, device_id_type=MESH,
            ).wait_recv()
        total += r3[:, k]
    total = jnp.concatenate([total[0], total[1]], axis=1)
    mine[...] = jnp.where(lax.rem(zh, 2) == 0, total[:, :192], total[:, 64:])
    fourth = remote(mine, r4, beside)
    fourth.wait()
    u = mine[...] + r4[...]

    def kept(k, m):
        return u[27 * k - 1 + m : 27 * k + m]

    fifth = []
    for k in range(1, 8):
        ends[k - 1, :9] = jnp.concatenate([kept(e, 3 * k + t) for t in range(3) for e in (1, 2, 0)], axis=0)
        fifth.append(remote(ends.at[k - 1], r5.at[k - 1], triple(k)))
    for c in fifth:
        c.wait()
    turned = []
    for t in range(3):
        k = TURN.index(t)
        rows = [u[27 * k - 1 : 27 * k + 26]] if k else [kept(1, 2), u[0:26]]
        rows += [r5[6 - e, 3 * t : 3 * t + 3] for e in range(7)]
        turned.append(pltpu.roll(jnp.concatenate(rows, axis=0), 3 * q, 0))
    low = jnp.concatenate([turned[0], turned[1][:24]], axis=0)
    top = jnp.concatenate([turned[1][24:], turned[2]], axis=0)
    o_ref[...] = jnp.where(zl == 0, low, top)


def ladder(x, b):
    slabs = pltpu.VMEM((3, 4, 4, 2, SLAB, 128), F32)
    return pl.pallas_call(
        ladder_kernel,
        out_shape=jax.ShapeDtypeStruct((ROWS, 192), F32),
        in_specs=[pl.BlockSpec(memory_space=pl.ANY)] * 2,
        out_specs=pl.BlockSpec(memory_space=pltpu.VMEM),
        scratch_shapes=[
            pltpu.VMEM((3, THIRD, O, 384), F32),
            pltpu.VMEM((DEPTH, COLS), F32),
            pltpu.VMEM((8 * PITCH, 128), F32),
            slabs,
            slabs,
            slabs,
            pltpu.VMEM((4, 4, 2, 3, SLAB, 128), F32),
            pltpu.VMEM((PAIRS, 128), F32),
            pltpu.VMEM((UNIQUE, WIDE), BF16),
            pltpu.VMEM((UNIQUE, WIDE), BF16),
            pltpu.VMEM((6, DEPTH, 256), BF16),
            pltpu.VMEM((6, DEPTH, 256), BF16),
            pltpu.VMEM((3, UNIQUE, 256), F32),
            pltpu.VMEM((3, UNIQUE, 256), F32),
            pltpu.VMEM((6, UNIQUE, 128), F32),
            pltpu.VMEM((6, 3, 4 * KEPT, 128), F32),
            pltpu.VMEM((6, 4 * KEPT, 128), F32),
            pltpu.VMEM((6, 3, KEPT, 128), F32),
            pltpu.VMEM((6, KEPT, 128), F32),
            pltpu.VMEM((2, 3, KEPT, 128), F32),
            pltpu.VMEM((KEPT, 192), F32),
            pltpu.VMEM((KEPT, 192), F32),
            pltpu.VMEM((7, 16, 192), F32),
            pltpu.VMEM((7, 16, 192), F32),
            pltpu.SemaphoreType.DMA((145,)),
            pltpu.SemaphoreType.DMA((145,)),
            pltpu.SemaphoreType.DMA((27,)),
            pltpu.SemaphoreType.DMA((4,)),
            pltpu.SemaphoreType.DMA((2, 3)),
        ],
        compiler_params=pltpu.CompilerParams(collective_id=0, has_side_effects=True, vmem_limit_bytes=62 << 20),
    )(x, b)


def on_device(amplitudes, integrals):
    slab_matrix = integrals.transpose(1, 0, 2).reshape(DEPTH, COLS)
    return ladder(amplitudes, slab_matrix)


def solution(mesh):
    in_specs = (P("occ", "vir", None), P("vir", "occ", None))
    out_specs = P("occ", "vir")
    return jax.shard_map(
        on_device, mesh=mesh, in_specs=in_specs, out_specs=out_specs, check_vma=False
    )
```

```python
import functools

import jax
import jax.numpy as jnp
from jax import lax
from jax.experimental import pallas as pl
from jax.experimental.pallas import tpu as pltpu
from jax.sharding import PartitionSpec as P

O = 48
MESH = pl.DeviceIdType.MESH
F32, BF16 = jnp.float32, jnp.bfloat16
SIZE = {"y": 4, "x": 4, "z": 2}
AXIS = {"y": 0, "x": 1, "z": 2}
ORDERS = (("y", "x", "z"), ("x", "z", "y"), ("z", "y", "x"))
ROWS, DEPTH, WIDE, COLS = 72, 576, 640, 1536
PAIRS = 2304


def occ_place():
    r = lax.axis_index("occ")
    return {"y": r // 8, "x": lax.rem(r // 2, 4), "z": lax.rem(r, 2)}


def occ_peer(me, dim, k):
    c = dict(me)
    c[dim] = lax.rem(me[dim] + k, SIZE[dim])
    return c[dim], c["y"] * 8 + c["x"] * 2 + c["z"]


THIRD = ROWS // 3
BLOCK_AT = (0, 32, 72, 112)
SLAB = BLOCK_AT[3]
PITCH = 392

TURN = (2, 0, 1)
KEPT = 80
UNIQUE = 16 * KEPT
CHUNK = 640


def split(x):
    hi = x.astype(BF16)
    return hi, (x - hi.astype(F32)).astype(BF16)


def ladder_kernel(
    x_ref, b_any, o_ref,
    x, b_ref, turned, g0, g1, g2, g3, rest, s_hi, s_lo, b_hi, b_lo,
    away, other, acc, r1, s1, r2, s2, r3, mine, r4, ends, r5,
    ssem, rsem, lsem, xsem, zsem,
):
    v = lax.axis_index("vir")
    r = lax.axis_index("occ")
    core, zh = lax.rem(v, 2), v // 2
    me = occ_place()
    q, zl = r // 2, me["z"]
    reads = [pltpu.make_async_copy(x_ref.at[pl.ds(t * THIRD, THIRD)], x.at[t], xsem.at[t]) for t in range(3)]
    reads.append(pltpu.make_async_copy(b_any, b_ref, xsem.at[3]))
    for c in reads:
        c.start()

    def triple(k):
        return (lax.rem(q + k, 16) * 2 + zl, v)

    twin = (r, v + 1 - 2 * core)
    beside = (r + 1 - 2 * zl, v)
    devices = [twin, beside] + [triple(k) for k in range(1, 16)] + [(r, lax.rem(zh + k, 4) * 2 + core) for k in range(1, 4)]
    barrier = pltpu.get_barrier_semaphore()
    for d in devices:
        pl.semaphore_signal(barrier, inc=1, device_id=d, device_id_type=MESH)

    sent = [0, 0]

    def remote(src, dst, device):
        n = sent[0]
        sent[0] += 1
        c = pltpu.make_async_remote_copy(
            src_ref=src, dst_ref=dst, send_sem=ssem.at[n], recv_sem=rsem.at[n], device_id=device, device_id_type=MESH
        )
        c.start()
        return c

    lane = lax.broadcasted_iota(jnp.int32, (8, 128), 1)

    def regroup(t, block):
        @pl.loop(0, 8, unroll=8)
        def _(p):
            turned[pl.ds(pl.multiple_of(p * PITCH, 8), 384), 0:O] = x[t, block * 8 + p].T

        @pl.loop(0, 32, unroll=8)
        def _(to):
            at = (t, to // 8, lax.rem(to // 2, 4), lax.rem(to, 2))
            tiles = [jnp.zeros((8, 128), F32)] * 5
            for d in range(12):
                tile, off = d * O // 128, d * O % 128
                piece = turned[pl.ds(to * 12 + d, 8, stride=PITCH), :]
                if off:
                    piece = pltpu.roll(piece, off, 1)
                tiles[tile] = jnp.where((lane >= off) & (lane < off + O), piece, tiles[tile])
                if off + O > 128:
                    tiles[tile + 1] = jnp.where(lane < off + O - 128, piece, tiles[tile + 1])
            for n in range(4):
                g0[(*at, slice(BLOCK_AT[block] + 8 * n, BLOCK_AT[block] + 8 * n + 8))] = tiles[n]
            behind = (*at, slice(64, 72) if block < 2 else slice(104, 112))
            if block == 1:
                g0[behind] = jnp.where(lane < 64, g0[behind], pltpu.roll(tiles[4], 64, 1))
            else:
                g0[behind] = tiles[4]

    def view(ref, t, dim, at, rows):
        ix = [slice(None)] * 3
        ix[AXIS[dim]] = at
        if ref is g3:
            return ref.at[ix[0], ix[1], ix[2], t, rows]
        return ref.at[t, ix[0], ix[1], ix[2], rows]

    held = [g0, g1, g2, g3]

    def start(t, s, block):
        dim = ORDERS[t][s]
        rows = pl.ds(BLOCK_AT[block], BLOCK_AT[block + 1] - BLOCK_AT[block])
        src, dst = held[s], held[s + 1]
        copies = []
        for k in range(1, SIZE[dim]):
            at, rank = occ_peer(me, dim, k)
            copies.append(remote(view(src, t, dim, at, rows), view(dst, t, dim, me[dim], rows), (rank, v)))
        own = pltpu.make_async_copy(
            view(src, t, dim, me[dim], rows), view(dst, t, dim, me[dim], rows), lsem.at[sent[1]]
        )
        sent[1] += 1
        own.start()
        return copies + [own]

    flying = {}
    for block in range(3):
        for t in range(3):
            if block == 0:
                reads[t].wait()
            regroup(t, block)
            if block == t == 0:
                pl.semaphore_wait(barrier, len(devices))
            flying[t, block] = start(t, 0, block)

    def onward(s):
        for block in range(3):
            for t in range(3):
                for c in flying[t, block]:
                    c.wait()
                if s < 3:
                    flying[t, block] = start(t, s, block)

    onward(1)

    reads[3].wait()

    @pl.loop(0, DEPTH // 48)
    def _(k):
        rows = pl.ds(pl.multiple_of(k * 48, 16), 48)
        b = b_ref[rows, :]
        for c in range(2):
            piece = jnp.concatenate([b[:, e * 384 + c * 192 : e * 384 + c * 192 + 192] for e in range(4)], axis=1)
            for n in range(3):
                b_hi[c * 3 + n, rows, :], b_lo[c * 3 + n, rows, :] = split(piece[:, n * 256 : (n + 1) * 256])

    onward(2)
    onward(3)

    flat = g3.reshape(32 * 3 * SLAB, 128)

    @pl.loop(0, PAIRS // THIRD, unroll=8)
    def _(g):
        both = flat[pl.ds(pl.multiple_of(g * SLAB + 64, 8), 8), :]
        rest[pl.ds(pl.multiple_of(g * THIRD, 8), 8), :] = both
        rest[pl.ds(pl.multiple_of(g * THIRD + 8, 8), 8), :] = pltpu.roll(both, 64, 1)
        rest[pl.ds(pl.multiple_of(g * THIRD + 16, 8), 8), :] = flat[pl.ds(pl.multiple_of(g * SLAB + 104, 8), 8), :]

    def place(t, p):
        return p // THIRD * SLAB + BLOCK_AT[p % THIRD // 8] + t * 8 + p % 8

    def straight(t, i, j, n):
        tiles = []
        for block in range(j // 8, (j + n + 7) // 8):
            p = i * O + block % 6 * 8
            tiles.append(rest[p : p + 8, :] if t == 4 else flat[pl.ds(place(t, p), 8), :])
        return jnp.concatenate(tiles, axis=0)[j % 8 : j % 8 + n]

    def mirrored(t, i, j, n):
        parts = []
        for first, count in ((j, min(n, O - j)), (0, n - min(n, O - j))):
            if count and t == 4:
                parts.append(rest[pl.ds(first * O + i, count, stride=O), :])
            elif count:
                parts.append(flat[pl.ds(place(t, first * O + i), count, stride=2 * SLAB), :])
        return jnp.concatenate(parts, axis=0)

    for t in range(5):
        for own in range(16):
            sums = []
            for k in range(3):
                i, m = 3 * own + TURN[k], int(k == 0)
                sums.append(straight(t, i, 3 * own + m, 27 - m) + mirrored(t, i, 3 * own + m, 27 - m))
            total = jnp.concatenate(sums, axis=0)
            if t == 4:
                total = jnp.where(lax.broadcasted_iota(jnp.int32, total.shape, 1) < 64, total, 0)
            at, lanes = slice(own * KEPT, (own + 1) * KEPT), slice(t * 128, (t + 1) * 128)
            s_hi[at, lanes], s_lo[at, lanes] = split(total)


    def product(n):
        @pl.loop(0, UNIQUE // CHUNK)
        def _(m):
            rows = pl.ds(pl.multiple_of(m * CHUNK, 128), CHUNK)
            dot = functools.partial(jnp.dot, preferred_element_type=F32)

            def multiply(at):
                hi, lo = s_hi[rows, :DEPTH], s_lo[rows, :DEPTH]
                return dot(hi, b_lo[at]) + dot(lo, b_hi[at]) + dot(hi, b_hi[at])

            if n >= 3:
                away[n - 3, rows, :] = multiply((1 - core) * 3 + n - 3)
            else:
                both = multiply(core * 3 + n)
                acc[2 * n, rows, :] = both[:, :128]
                acc[2 * n + 1, rows, :] = both[:, 128:]

    def ring(src, landing, dim, pieces):
        up, up_rank = occ_peer(me, dim, 1)
        down, down_rank = occ_peer(me, dim, 3)
        far, _ = occ_peer(me, dim, 2)

        def send(at, half, rank, slot):
            return [
                remote(src.at[pl.ds(begin, n)], landing.at[slot, pl.ds(to, n)], (rank, v))
                for begin, to, n in pieces(at, half)
            ]

        relays = send(far, 0, up_rank, 2) + send(far, 1, down_rank, 2)
        direct = send(up, 1, up_rank, 0) + send(down, 0, down_rank, 1)

        def forward():
            for c in relays:
                c.wait()
            for at, half in ((up, 0), (down, 1)):
                for begin, to, n in pieces(at, half):
                    src[pl.ds(begin, n), :] += landing[2, pl.ds(to, n), :]
            direct.extend(send(up, 0, up_rank, 0) + send(down, 1, down_rank, 1))

        def finish():
            for c in direct:
                c.wait()

        return forward, finish

    def of_y(at, half):
        return [(pl.multiple_of((at * 4 + 2 * half) * KEPT, 8), 2 * half * KEPT, 2 * KEPT)]

    def of_x(at, half):
        return [(pl.multiple_of((y * 4 + at) * KEPT, 8), y * KEPT, KEPT) for y in (2 * half, 2 * half + 1)]

    def of_rest(at, half):
        return [(pl.multiple_of(at * KEPT + half * (KEPT // 2), 8), half * (KEPT // 2), KEPT // 2)]

    swap, first, second = [], [], []
    for n in (3, 0, 4, 1, 5, 2):
        product(n)
        if n >= 3:
            swap.append(remote(away.at[n - 3], other.at[n - 3], twin))
            continue
        swap[n].wait()

        @pl.loop(0, 16)
        def _(m):
            rows = pl.ds(pl.multiple_of(m * KEPT, 8), KEPT)
            acc[2 * n, rows, :] += other[n, rows, :128]
            acc[2 * n + 1, rows, :] += other[n, rows, 128:]

        first += [ring(acc.at[e], r1.at[e], "yx"[e % 2], (of_y, of_x)[e % 2]) for e in (2 * n, 2 * n + 1)]
        if n:
            first[2 * n - 2][0]()
            first[2 * n - 1][0]()
    first[4][0]()
    first[5][0]()

    for n in range(3):
        for e in (2 * n, 2 * n + 1):
            first[e][1]()
            for y in range(4):
                part = pl.ds(y * KEPT, KEPT)
                base = (me["y"] * 4 + y) if e % 2 == 0 else (y * 4 + me["x"])
                own = pl.ds(pl.multiple_of(base * KEPT, 8), KEPT)
                s1[e, part, :] = acc[e, own, :] + (r1[e, 0, part, :] + r1[e, 1, part, :])
            second.append(ring(s1.at[e], r2.at[e], "xy"[e % 2], of_rest))
        if n:
            second[2 * n - 2][0]()
            second[2 * n - 1][0]()
    second[4][0]()
    second[5][0]()

    third = []
    for n in range(3):
        for h in range(2):
            e = 2 * n + h
            second[e][1]()
            own = pl.ds(pl.multiple_of(me["xy"[h]] * KEPT, 8), KEPT)
            s2[e] = s1[e, own, :] + (r2[e, 0] + r2[e, 1])
            for half in range(2):
                if e % 3 == 2 - 2 * half:
                    continue
                to = e // 3 * 2 + half
                slot, k = e % 3 - half, lax.rem(zh - to + 4, 4)
                c = pltpu.make_async_remote_copy(
                    src_ref=s2.at[e],
                    dst_ref=r3.at[slot, lax.max(k - 1, 0)],
                    send_sem=ssem.at[sent[0]],
                    recv_sem=zsem.at[slot, lax.max(k - 1, 0)],
                    device_id=(r, to * 2 + core),
                    device_id_type=MESH,
                )
                sent[0] += 1
                third.append((to, c))
                pl.when(zh != to)(c.start)
    for to, c in third:
        pl.when(zh != to)(c.wait_send)
    total = s2[pl.ds(zh // 2 * 3 + lax.rem(zh, 2), 2)]
    for k in range(3):
        for slot in range(2):
            pltpu.make_async_remote_copy(
                src_ref=s2.at[slot], dst_ref=r3.at[slot, k], send_sem=ssem.at[0], recv_sem=zsem.at[slot, k],
                device_id=twin, device_id_type=MESH,
            ).wait_recv()
        total += r3[:, k]
    total = jnp.concatenate([total[0], total[1]], axis=1)
    mine[...] = jnp.where(lax.rem(zh, 2) == 0, total[:, :192], total[:, 64:])
    fourth = remote(mine, r4, beside)
    fourth.wait()
    u = mine[...] + r4[...]

    def kept(k, m):
        return u[27 * k - 1 + m : 27 * k + m]

    fifth = []
    for k in range(1, 8):
        ends[k - 1, :9] = jnp.concatenate([kept(e, 3 * k + t) for t in range(3) for e in (1, 2, 0)], axis=0)
        fifth.append(remote(ends.at[k - 1], r5.at[k - 1], triple(k)))
    for c in fifth:
        c.wait()
    turned = []
    for t in range(3):
        k = TURN.index(t)
        rows = [u[27 * k - 1 : 27 * k + 26]] if k else [kept(1, 2), u[0:26]]
        rows += [r5[6 - e, 3 * t : 3 * t + 3] for e in range(7)]
        turned.append(pltpu.roll(jnp.concatenate(rows, axis=0), 3 * q, 0))
    low = jnp.concatenate([turned[0], turned[1][:24]], axis=0)
    top = jnp.concatenate([turned[1][24:], turned[2]], axis=0)
    o_ref[...] = jnp.where(zl == 0, low, top)


def ladder(x, b):
    slabs = pltpu.VMEM((3, 4, 4, 2, SLAB, 128), F32)
    return pl.pallas_call(
        ladder_kernel,
        out_shape=jax.ShapeDtypeStruct((ROWS, 192), F32),
        in_specs=[pl.BlockSpec(memory_space=pl.ANY)] * 2,
        out_specs=pl.BlockSpec(memory_space=pltpu.VMEM),
        scratch_shapes=[
            pltpu.VMEM((3, THIRD, O, 384), F32),
            pltpu.VMEM((DEPTH, COLS), F32),
            pltpu.VMEM((8 * PITCH, 128), F32),
            slabs,
            slabs,
            slabs,
            pltpu.VMEM((4, 4, 2, 3, SLAB, 128), F32),
            pltpu.VMEM((PAIRS, 128), F32),
            pltpu.VMEM((UNIQUE, WIDE), BF16),
            pltpu.VMEM((UNIQUE, WIDE), BF16),
            pltpu.VMEM((6, DEPTH, 256), BF16),
            pltpu.VMEM((6, DEPTH, 256), BF16),
            pltpu.VMEM((3, UNIQUE, 256), F32),
            pltpu.VMEM((3, UNIQUE, 256), F32),
            pltpu.VMEM((6, UNIQUE, 128), F32),
            pltpu.VMEM((6, 3, 4 * KEPT, 128), F32),
            pltpu.VMEM((6, 4 * KEPT, 128), F32),
            pltpu.VMEM((6, 3, KEPT, 128), F32),
            pltpu.VMEM((6, KEPT, 128), F32),
            pltpu.VMEM((2, 3, KEPT, 128), F32),
            pltpu.VMEM((KEPT, 192), F32),
            pltpu.VMEM((KEPT, 192), F32),
            pltpu.VMEM((7, 16, 192), F32),
            pltpu.VMEM((7, 16, 192), F32),
            pltpu.SemaphoreType.DMA((172,)),
            pltpu.SemaphoreType.DMA((172,)),
            pltpu.SemaphoreType.DMA((27,)),
            pltpu.SemaphoreType.DMA((4,)),
            pltpu.SemaphoreType.DMA((2, 3)),
        ],
        compiler_params=pltpu.CompilerParams(collective_id=0, has_side_effects=True, vmem_limit_bytes=62 << 20),
    )(x, b)


def on_device(amplitudes, integrals):
    slab_matrix = integrals.transpose(1, 0, 2).reshape(DEPTH, COLS)
    return ladder(amplitudes, slab_matrix)


def solution(mesh):
    in_specs = (P("occ", "vir", None), P("vir", "occ", None))
    out_specs = P("occ", "vir")
    return jax.shard_map(
        on_device, mesh=mesh, in_specs=in_specs, out_specs=out_specs, check_vma=False
    )
```

```python
import jax
import jax.numpy as jnp
from jax import lax
from jax.experimental import pallas as pl
from jax.experimental.pallas import tpu as pltpu
from jax.sharding import PartitionSpec as P

O = 48
MESH = pl.DeviceIdType.MESH
F32, BF16 = jnp.float32, jnp.bfloat16
SIZE = {"y": 4, "x": 4, "z": 2}
AXIS = {"y": 0, "x": 1, "z": 2}
ORDERS = (("y", "x", "z"), ("x", "z", "y"), ("z", "y", "x"))
ROWS, DEPTH, COLS = 72, 576, 1536
PAIRS = 2304


def occ_place():
    r = lax.axis_index("occ")
    return {"y": r // 8, "x": lax.rem(r // 2, 4), "z": lax.rem(r, 2)}


def occ_peer(me, dim, k):
    c = dict(me)
    c[dim] = lax.rem(me[dim] + k, SIZE[dim])
    return c[dim], c["y"] * 8 + c["x"] * 2 + c["z"]


THIRD = ROWS // 3
BLOCK_AT = (0, 32, 72, 112)
SLAB = BLOCK_AT[3]
PITCH = 392

TURN = (2, 0, 1)
KEPT = 80
UNIQUE = 16 * KEPT
CHUNK = 640


def split(x):
    hi = x.astype(BF16)
    return hi, (x - hi.astype(F32)).astype(BF16)


def ladder_kernel(
    x_ref, b_any, o_ref,
    x, b_ref, turned, g0, g1, g2, g3, rest, s_hi, s_lo, s_mix, b_hi, b_lo,
    away, other, acc, r1, s1, r2, s2, r3, mine, r4, ends, r5,
    ssem, rsem, lsem, xsem, zsem,
):
    v = lax.axis_index("vir")
    r = lax.axis_index("occ")
    core, zh = lax.rem(v, 2), v // 2
    me = occ_place()
    q, zl = r // 2, me["z"]
    reads = {}
    for block in range(3):
        for t in range(3):
            rows = pl.ds(t * THIRD + block * 8, 8)
            reads[t, block] = pltpu.make_async_copy(
                x_ref.at[rows], x.at[t, pl.ds(block * 8, 8)], xsem.at[block * 3 + t]
            )
            reads[t, block].start()
    read_b = pltpu.make_async_copy(b_any, b_ref, xsem.at[9])

    def triple(k):
        return (lax.rem(q + k, 16) * 2 + zl, v)

    twin = (r, v + 1 - 2 * core)
    beside = (r + 1 - 2 * zl, v)
    devices = [twin, beside] + [triple(k) for k in range(1, 16)] + [(r, lax.rem(zh + k, 4) * 2 + core) for k in range(1, 4)]
    barrier = pltpu.get_barrier_semaphore()
    for d in devices:
        pl.semaphore_signal(barrier, inc=1, device_id=d, device_id_type=MESH)

    sent = [0, 0]

    def remote(src, dst, device):
        n = sent[0]
        sent[0] += 1
        c = pltpu.make_async_remote_copy(
            src_ref=src, dst_ref=dst, send_sem=ssem.at[n], recv_sem=rsem.at[n], device_id=device, device_id_type=MESH
        )
        c.start()
        return c

    lane = lax.broadcasted_iota(jnp.int32, (8, 128), 1)

    def regroup(t, block):
        @pl.loop(0, 8, unroll=8)
        def _(p):
            turned[pl.ds(pl.multiple_of(p * PITCH, 8), 384), 0:O] = x[t, block * 8 + p].T

        @pl.loop(0, 32, unroll=8)
        def _(to):
            at = (t, to // 8, lax.rem(to // 2, 4), lax.rem(to, 2))
            tiles = [jnp.zeros((8, 128), F32)] * 5
            for d in range(12):
                tile, off = d * O // 128, d * O % 128
                piece = turned[pl.ds(to * 12 + d, 8, stride=PITCH), :]
                if off:
                    piece = pltpu.roll(piece, off, 1)
                tiles[tile] = jnp.where((lane >= off) & (lane < off + O), piece, tiles[tile])
                if off + O > 128:
                    tiles[tile + 1] = jnp.where(lane < off + O - 128, piece, tiles[tile + 1])
            for n in range(4):
                g0[(*at, slice(BLOCK_AT[block] + 8 * n, BLOCK_AT[block] + 8 * n + 8))] = tiles[n]
            behind = (*at, slice(64, 72) if block < 2 else slice(104, 112))
            if block == 1:
                g0[behind] = jnp.where(lane < 64, g0[behind], pltpu.roll(tiles[4], 64, 1))
            else:
                g0[behind] = tiles[4]

    def view(ref, t, dim, at, rows):
        ix = [slice(None)] * 3
        ix[AXIS[dim]] = at
        if ref is g3:
            return ref.at[ix[0], ix[1], ix[2], t, rows]
        return ref.at[t, ix[0], ix[1], ix[2], rows]

    held = [g0, g1, g2, g3]

    def start(t, s, block):
        dim = ORDERS[t][s]
        rows = pl.ds(BLOCK_AT[block], BLOCK_AT[block + 1] - BLOCK_AT[block])
        src, dst = held[s], held[s + 1]
        copies = []
        for k in range(1, SIZE[dim]):
            at, rank = occ_peer(me, dim, k)
            copies.append(remote(view(src, t, dim, at, rows), view(dst, t, dim, me[dim], rows), (rank, v)))
        own = pltpu.make_async_copy(
            view(src, t, dim, me[dim], rows), view(dst, t, dim, me[dim], rows), lsem.at[sent[1]]
        )
        sent[1] += 1
        own.start()
        return copies + [own]

    flying = {}
    for block in range(3):
        for t in range(3):
            reads[t, block].wait()
            regroup(t, block)
            if block == t == 0:
                read_b.start()
                pl.semaphore_wait(barrier, len(devices))
            flying[t, block] = start(t, 0, block)

    def onward(s):
        for block in range(3):
            for t in range(3):
                for c in flying[t, block]:
                    c.wait()
                if s < 3:
                    flying[t, block] = start(t, s, block)

    onward(1)

    read_b.wait()

    @pl.loop(0, DEPTH // 48)
    def _(k):
        rows = pl.ds(pl.multiple_of(k * 48, 16), 48)
        b = b_ref[rows, :]
        for c in range(2):
            piece = jnp.concatenate([b[:, e * 384 + c * 192 : e * 384 + c * 192 + 192] for e in range(4)], axis=1)
            for n in range(3):
                b_hi[c * 3 + n, rows, :], b_lo[c * 3 + n, rows, :] = split(piece[:, n * 256 : (n + 1) * 256])

    onward(2)
    onward(3)

    flat = g3.reshape(32 * 3 * SLAB, 128)

    @pl.loop(0, PAIRS // THIRD, unroll=8)
    def _(g):
        both = flat[pl.ds(pl.multiple_of(g * SLAB + 64, 8), 8), :]
        rest[pl.ds(pl.multiple_of(g * THIRD, 8), 8), :] = both
        rest[pl.ds(pl.multiple_of(g * THIRD + 8, 8), 8), :] = pltpu.roll(both, 64, 1)
        rest[pl.ds(pl.multiple_of(g * THIRD + 16, 8), 8), :] = flat[pl.ds(pl.multiple_of(g * SLAB + 104, 8), 8), :]

    def place(t, p):
        return p // THIRD * SLAB + BLOCK_AT[p % THIRD // 8] + t * 8 + p % 8

    def straight(t, i, j, n):
        tiles = []
        for block in range(j // 8, (j + n + 7) // 8):
            p = i * O + block % 6 * 8
            tiles.append(rest[p : p + 8, :] if t == 4 else flat[pl.ds(place(t, p), 8), :])
        return jnp.concatenate(tiles, axis=0)[j % 8 : j % 8 + n]

    def mirrored(t, i, j, n):
        parts = []
        for first, count in ((j, min(n, O - j)), (0, n - min(n, O - j))):
            if count and t == 4:
                parts.append(rest[pl.ds(first * O + i, count, stride=O), :])
            elif count:
                parts.append(flat[pl.ds(place(t, first * O + i), count, stride=2 * SLAB), :])
        return jnp.concatenate(parts, axis=0)

    for t in range(5):
        for own in range(16):
            sums = []
            for k in range(3):
                i, m = 3 * own + TURN[k], int(k == 0)
                sums.append(straight(t, i, 3 * own + m, 27 - m) + mirrored(t, i, 3 * own + m, 27 - m))
            total = jnp.concatenate(sums, axis=0)
            at, lanes = slice(own * KEPT, (own + 1) * KEPT), slice(t * 128, (t + 1) * 128)
            if t < 4:
                s_hi[at, lanes], s_lo[at, lanes] = split(total)
            else:
                high = total.astype(BF16).astype(F32)
                low = pltpu.roll(total - high, 64, 1)
                left = lax.broadcasted_iota(jnp.int32, total.shape, 1) < 64
                s_mix[at, :] = jnp.where(left, high, low).astype(BF16)


    def product(n):
        @pl.loop(0, UNIQUE // CHUNK)
        def _(m):
            rows = pl.ds(pl.multiple_of(m * CHUNK, 128), CHUNK)

            def multiply(at):
                hi, lo, mix = s_hi[rows, :], s_lo[rows, :], s_mix[rows, :]
                hi_top, hi_end = b_hi[at, :512], b_hi[at, 512:]
                lo_top, lo_end = b_lo[at, :512], b_lo[at, 512:]
                none = jnp.zeros_like(lo_end)
                return jnp.dot(
                    jnp.concatenate([hi, mix, lo, hi, mix], axis=1),
                    jnp.concatenate([hi_top, hi_end, hi_end, hi_top, lo_top, lo_end, none], axis=0),
                    preferred_element_type=F32,
                )

            if n >= 3:
                away[n - 3, rows, :] = multiply((1 - core) * 3 + n - 3)
            else:
                both = multiply(core * 3 + n)
                acc[2 * n, rows, :] = both[:, :128]
                acc[2 * n + 1, rows, :] = both[:, 128:]

    def ring(src, landing, dim, pieces):
        up, up_rank = occ_peer(me, dim, 1)
        down, down_rank = occ_peer(me, dim, 3)
        far, _ = occ_peer(me, dim, 2)

        def send(at, half, rank, slot):
            return [
                remote(src.at[pl.ds(begin, n)], landing.at[slot, pl.ds(to, n)], (rank, v))
                for begin, to, n in pieces(at, half)
            ]

        relays = send(far, 0, up_rank, 2) + send(far, 1, down_rank, 2)
        direct = send(up, 1, up_rank, 0) + send(down, 0, down_rank, 1)

        def forward():
            for c in relays:
                c.wait()
            for at, half in ((up, 0), (down, 1)):
                for begin, to, n in pieces(at, half):
                    src[pl.ds(begin, n), :] += landing[2, pl.ds(to, n), :]
            direct.extend(send(up, 0, up_rank, 0) + send(down, 1, down_rank, 1))

        def finish():
            for c in direct:
                c.wait()

        return forward, finish

    def of_y(at, half):
        return [(pl.multiple_of((at * 4 + 2 * half) * KEPT, 8), 2 * half * KEPT, 2 * KEPT)]

    def of_x(at, half):
        return [(pl.multiple_of((y * 4 + at) * KEPT, 8), y * KEPT, KEPT) for y in (2 * half, 2 * half + 1)]

    swap, first, second = [], [], []
    for n in (3, 0, 4, 1, 5, 2):
        product(n)
        if n >= 3:
            swap.append(remote(away.at[n - 3], other.at[n - 3], twin))
            continue
        swap[n].wait()

        @pl.loop(0, 16)
        def _(m):
            rows = pl.ds(pl.multiple_of(m * KEPT, 8), KEPT)
            acc[2 * n, rows, :] += other[n, rows, :128]
            acc[2 * n + 1, rows, :] += other[n, rows, 128:]

        first += [ring(acc.at[e], r1.at[e], "yx"[e % 2], (of_y, of_x)[e % 2]) for e in (2 * n, 2 * n + 1)]
        if n:
            first[2 * n - 2][0]()
            first[2 * n - 1][0]()
    first[4][0]()
    first[5][0]()

    for n in range(3):
        for e in (2 * n, 2 * n + 1):
            first[e][1]()
            for y in range(4):
                part = pl.ds(y * KEPT, KEPT)
                base = (me["y"] * 4 + y) if e % 2 == 0 else (y * 4 + me["x"])
                own = pl.ds(pl.multiple_of(base * KEPT, 8), KEPT)
                s1[e, part, :] = acc[e, own, :] + (r1[e, 0, part, :] + r1[e, 1, part, :])
            copies = []
            for k in range(1, 4):
                at, rank = occ_peer(me, "xy"[e % 2], k)
                rows = pl.ds(pl.multiple_of(at * KEPT, 8), KEPT)
                copies.append(remote(s1.at[e, rows], r2.at[e, k - 1], (rank, v)))
            second.append(copies)

    third = []
    for n in range(3):
        for h in range(2):
            e = 2 * n + h
            for c in second[e]:
                c.wait()
            own = pl.ds(pl.multiple_of(me["xy"[h]] * KEPT, 8), KEPT)
            s2[e] = (s1[e, own, :] + r2[e, 0]) + (r2[e, 1] + r2[e, 2])
            for half in range(2):
                if e % 3 == 2 - 2 * half:
                    continue
                to = e // 3 * 2 + half
                slot, k = e % 3 - half, lax.rem(zh - to + 4, 4)
                c = pltpu.make_async_remote_copy(
                    src_ref=s2.at[e],
                    dst_ref=r3.at[slot, lax.max(k - 1, 0)],
                    send_sem=ssem.at[sent[0]],
                    recv_sem=zsem.at[slot, lax.max(k - 1, 0)],
                    device_id=(r, to * 2 + core),
                    device_id_type=MESH,
                )
                sent[0] += 1
                third.append((to, c))
                pl.when(zh != to)(c.start)
    for to, c in third:
        pl.when(zh != to)(c.wait_send)
    total = s2[pl.ds(zh // 2 * 3 + lax.rem(zh, 2), 2)]
    for k in range(3):
        for slot in range(2):
            pltpu.make_async_remote_copy(
                src_ref=s2.at[slot], dst_ref=r3.at[slot, k], send_sem=ssem.at[0], recv_sem=zsem.at[slot, k],
                device_id=twin, device_id_type=MESH,
            ).wait_recv()
        total += r3[:, k]
    total = jnp.concatenate([total[0], total[1]], axis=1)
    mine[...] = jnp.where(lax.rem(zh, 2) == 0, total[:, :192], total[:, 64:])
    fourth = remote(mine, r4, beside)
    fourth.wait()
    u = mine[...] + r4[...]

    def kept(k, m):
        return u[27 * k - 1 + m : 27 * k + m]

    fifth = []
    for k in range(1, 8):
        ends[k - 1, :9] = jnp.concatenate([kept(e, 3 * k + t) for t in range(3) for e in (1, 2, 0)], axis=0)
        fifth.append(remote(ends.at[k - 1], r5.at[k - 1], triple(k)))
    for c in fifth:
        c.wait()
    turned = []
    for t in range(3):
        k = TURN.index(t)
        rows = [u[27 * k - 1 : 27 * k + 26]] if k else [kept(1, 2), u[0:26]]
        rows += [r5[6 - e, 3 * t : 3 * t + 3] for e in range(7)]
        turned.append(pltpu.roll(jnp.concatenate(rows, axis=0), 3 * q, 0))
    low = jnp.concatenate([turned[0], turned[1][:24]], axis=0)
    top = jnp.concatenate([turned[1][24:], turned[2]], axis=0)
    o_ref[...] = jnp.where(zl == 0, low, top)


def ladder(x, b):
    slabs = pltpu.VMEM((3, 4, 4, 2, SLAB, 128), F32)
    return pl.pallas_call(
        ladder_kernel,
        out_shape=jax.ShapeDtypeStruct((ROWS, 192), F32),
        in_specs=[pl.BlockSpec(memory_space=pl.ANY)] * 2,
        out_specs=pl.BlockSpec(memory_space=pltpu.VMEM),
        scratch_shapes=[
            pltpu.VMEM((3, THIRD, O, 384), F32),
            pltpu.VMEM((DEPTH, COLS), F32),
            pltpu.VMEM((8 * PITCH, 128), F32),
            slabs,
            slabs,
            slabs,
            pltpu.VMEM((4, 4, 2, 3, SLAB, 128), F32),
            pltpu.VMEM((PAIRS, 128), F32),
            pltpu.VMEM((UNIQUE, 512), BF16),
            pltpu.VMEM((UNIQUE, 512), BF16),
            pltpu.VMEM((UNIQUE, 128), BF16),
            pltpu.VMEM((6, DEPTH, 256), BF16),
            pltpu.VMEM((6, DEPTH, 256), BF16),
            pltpu.VMEM((3, UNIQUE, 256), F32),
            pltpu.VMEM((3, UNIQUE, 256), F32),
            pltpu.VMEM((6, UNIQUE, 128), F32),
            pltpu.VMEM((6, 3, 4 * KEPT, 128), F32),
            pltpu.VMEM((6, 4 * KEPT, 128), F32),
            pltpu.VMEM((6, 3, KEPT, 128), F32),
            pltpu.VMEM((6, KEPT, 128), F32),
            pltpu.VMEM((2, 3, KEPT, 128), F32),
            pltpu.VMEM((KEPT, 192), F32),
            pltpu.VMEM((KEPT, 192), F32),
            pltpu.VMEM((7, 16, 192), F32),
            pltpu.VMEM((7, 16, 192), F32),
            pltpu.SemaphoreType.DMA((154,)),
            pltpu.SemaphoreType.DMA((154,)),
            pltpu.SemaphoreType.DMA((27,)),
            pltpu.SemaphoreType.DMA((10,)),
            pltpu.SemaphoreType.DMA((2, 3)),
        ],
        compiler_params=pltpu.CompilerParams(collective_id=0, has_side_effects=True, vmem_limit_bytes=62 << 20),
    )(x, b)


def on_device(amplitudes, integrals):
    slab_matrix = integrals.transpose(1, 0, 2).reshape(DEPTH, COLS)
    return ladder(amplitudes, slab_matrix)


def solution(mesh):
    in_specs = (P("occ", "vir", None), P("vir", "occ", None))
    out_specs = P("occ", "vir")
    return jax.shard_map(
        on_device, mesh=mesh, in_specs=in_specs, out_specs=out_specs, check_vma=False
    )
```

```python
import jax
import jax.numpy as jnp
from jax import lax
from jax.experimental import pallas as pl
from jax.experimental.pallas import tpu as pltpu
from jax.sharding import PartitionSpec as P

O = 48
MESH = pl.DeviceIdType.MESH
F32, BF16 = jnp.float32, jnp.bfloat16
SIZE = {"y": 4, "x": 4, "z": 2}
AXIS = {"y": 0, "x": 1, "z": 2}
ORDERS = (("y", "x", "z"), ("x", "z", "y"), ("z", "y", "x"))
ROWS, DEPTH, COLS = 72, 576, 1536
PAIRS = 2304


def occ_place():
    r = lax.axis_index("occ")
    return {"y": r // 8, "x": lax.rem(r // 2, 4), "z": lax.rem(r, 2)}


def occ_peer(me, dim, k):
    c = dict(me)
    c[dim] = lax.rem(me[dim] + k, SIZE[dim])
    return c[dim], c["y"] * 8 + c["x"] * 2 + c["z"]


THIRD = ROWS // 3
BLOCK_AT = (0, 32, 72, 112)
SLAB = BLOCK_AT[3]
PITCH = 392

TURN = (2, 0, 1)
KEPT = 80
UNIQUE = 16 * KEPT
CHUNK = 640


def split(x):
    hi = x.astype(BF16)
    return hi, (x - hi.astype(F32)).astype(BF16)


def ladder_kernel(
    x_ref, b_any, o_ref,
    x, b_ref, turned, g0, g1, g2, g3, rest, s_hi, s_lo, s_mix, b_hi, b_lo,
    away, other, acc, r1, s1, r2, s2, r3, mine, r4, ends, r5,
    ssem, rsem, lsem, xsem, zsem,
):
    v = lax.axis_index("vir")
    r = lax.axis_index("occ")
    core, zh = lax.rem(v, 2), v // 2
    me = occ_place()
    q, zl = r // 2, me["z"]
    reads = {}
    for block in range(3):
        for t in range(3):
            rows = pl.ds(t * THIRD + block * 8, 8)
            reads[t, block] = pltpu.make_async_copy(
                x_ref.at[rows], x.at[t, pl.ds(block * 8, 8)], xsem.at[block * 3 + t]
            )
            reads[t, block].start()
    read_b = pltpu.make_async_copy(b_any, b_ref, xsem.at[9])

    def triple(k):
        return (lax.rem(q + k, 16) * 2 + zl, v)

    twin = (r, v + 1 - 2 * core)
    beside = (r + 1 - 2 * zl, v)
    devices = [twin, beside] + [triple(k) for k in range(1, 16)] + [(r, lax.rem(zh + k, 4) * 2 + core) for k in range(1, 4)]
    barrier = pltpu.get_barrier_semaphore()
    for d in devices:
        pl.semaphore_signal(barrier, inc=1, device_id=d, device_id_type=MESH)

    sent = [0, 0]

    def remote(src, dst, device):
        n = sent[0]
        sent[0] += 1
        c = pltpu.make_async_remote_copy(
            src_ref=src, dst_ref=dst, send_sem=ssem.at[n], recv_sem=rsem.at[n], device_id=device, device_id_type=MESH
        )
        c.start()
        return c

    lane = lax.broadcasted_iota(jnp.int32, (8, 128), 1)

    def regroup(t, block):
        @pl.loop(0, 8, unroll=8)
        def _(p):
            turned[pl.ds(pl.multiple_of(p * PITCH, 8), 384), 0:O] = x[t, block * 8 + p].T

        @pl.loop(0, 32, unroll=8)
        def _(to):
            at = (t, to // 8, lax.rem(to // 2, 4), lax.rem(to, 2))
            tiles = [jnp.zeros((8, 128), F32)] * 5
            for d in range(12):
                tile, off = d * O // 128, d * O % 128
                piece = turned[pl.ds(to * 12 + d, 8, stride=PITCH), :]
                if off:
                    piece = pltpu.roll(piece, off, 1)
                tiles[tile] = jnp.where((lane >= off) & (lane < off + O), piece, tiles[tile])
                if off + O > 128:
                    tiles[tile + 1] = jnp.where(lane < off + O - 128, piece, tiles[tile + 1])
            for n in range(4):
                g0[(*at, slice(BLOCK_AT[block] + 8 * n, BLOCK_AT[block] + 8 * n + 8))] = tiles[n]
            behind = (*at, slice(64, 72) if block < 2 else slice(104, 112))
            if block == 1:
                g0[behind] = jnp.where(lane < 64, g0[behind], pltpu.roll(tiles[4], 64, 1))
            else:
                g0[behind] = tiles[4]

    def view(ref, t, dim, at, rows):
        ix = [slice(None)] * 3
        ix[AXIS[dim]] = at
        if ref is g3:
            return ref.at[ix[0], ix[1], ix[2], t, rows]
        return ref.at[t, ix[0], ix[1], ix[2], rows]

    held = [g0, g1, g2, g3]

    def start(t, s, block):
        dim = ORDERS[t][s]
        rows = pl.ds(BLOCK_AT[block], BLOCK_AT[block + 1] - BLOCK_AT[block])
        src, dst = held[s], held[s + 1]
        copies = []
        for k in range(1, SIZE[dim]):
            at, rank = occ_peer(me, dim, k)
            copies.append(remote(view(src, t, dim, at, rows), view(dst, t, dim, me[dim], rows), (rank, v)))
        own = pltpu.make_async_copy(
            view(src, t, dim, me[dim], rows), view(dst, t, dim, me[dim], rows), lsem.at[sent[1]]
        )
        sent[1] += 1
        own.start()
        return copies + [own]

    flying = {}
    for block in range(3):
        for t in range(3):
            reads[t, block].wait()
            regroup(t, block)
            if block == t == 0:
                read_b.start()
                pl.semaphore_wait(barrier, len(devices))
            flying[t, block] = start(t, 0, block)

    def onward(s):
        for block in range(3):
            for t in range(3):
                for c in flying[t, block]:
                    c.wait()
                if s < 3:
                    flying[t, block] = start(t, s, block)

    onward(1)

    read_b.wait()

    @pl.loop(0, DEPTH // 48)
    def _(k):
        rows = pl.ds(pl.multiple_of(k * 48, 16), 48)
        b = b_ref[rows, :]
        for c in range(2):
            piece = jnp.concatenate([b[:, e * 384 + c * 192 : e * 384 + c * 192 + 192] for e in range(4)], axis=1)
            for n in range(3):
                b_hi[c * 3 + n, rows, :], b_lo[c * 3 + n, rows, :] = split(piece[:, n * 256 : (n + 1) * 256])

    onward(2)
    onward(3)

    flat = g3.reshape(32 * 3 * SLAB, 128)

    @pl.loop(0, PAIRS // THIRD, unroll=8)
    def _(g):
        both = flat[pl.ds(pl.multiple_of(g * SLAB + 64, 8), 8), :]
        rest[pl.ds(pl.multiple_of(g * THIRD, 8), 8), :] = both
        rest[pl.ds(pl.multiple_of(g * THIRD + 8, 8), 8), :] = pltpu.roll(both, 64, 1)
        rest[pl.ds(pl.multiple_of(g * THIRD + 16, 8), 8), :] = flat[pl.ds(pl.multiple_of(g * SLAB + 104, 8), 8), :]

    def place(t, p):
        return p // THIRD * SLAB + BLOCK_AT[p % THIRD // 8] + t * 8 + p % 8

    def straight(t, i, j, n):
        tiles = []
        for block in range(j // 8, (j + n + 7) // 8):
            p = i * O + block % 6 * 8
            tiles.append(rest[p : p + 8, :] if t == 4 else flat[pl.ds(place(t, p), 8), :])
        return jnp.concatenate(tiles, axis=0)[j % 8 : j % 8 + n]

    def mirrored(t, i, j, n):
        parts = []
        for first, count in ((j, min(n, O - j)), (0, n - min(n, O - j))):
            if count and t == 4:
                parts.append(rest[pl.ds(first * O + i, count, stride=O), :])
            elif count:
                parts.append(flat[pl.ds(place(t, first * O + i), count, stride=2 * SLAB), :])
        return jnp.concatenate(parts, axis=0)

    for t in range(5):
        for own in range(16):
            sums = []
            for k in range(3):
                i, m = 3 * own + TURN[k], int(k == 0)
                sums.append(straight(t, i, 3 * own + m, 27 - m) + mirrored(t, i, 3 * own + m, 27 - m))
            total = jnp.concatenate(sums, axis=0)
            at, lanes = slice(own * KEPT, (own + 1) * KEPT), slice(t * 128, (t + 1) * 128)
            if t < 4:
                s_hi[at, lanes], s_lo[at, lanes] = split(total)
            else:
                high = total.astype(BF16).astype(F32)
                low = pltpu.roll(total - high, 64, 1)
                left = lax.broadcasted_iota(jnp.int32, total.shape, 1) < 64
                s_mix[at, :] = jnp.where(left, high, low).astype(BF16)


    def product(n):
        @pl.loop(0, UNIQUE // CHUNK)
        def _(m):
            rows = pl.ds(pl.multiple_of(m * CHUNK, 128), CHUNK)

            def multiply(at):
                hi, lo, mix = s_hi[rows, :], s_lo[rows, :], s_mix[rows, :]
                hi_top, hi_end = b_hi[at, :512], b_hi[at, 512:]
                lo_top, lo_end = b_lo[at, :512], b_lo[at, 512:]
                none = jnp.zeros_like(lo_end)
                return jnp.dot(
                    jnp.concatenate([hi, mix, lo, hi, mix], axis=1),
                    jnp.concatenate([hi_top, hi_end, hi_end, hi_top, lo_top, lo_end, none], axis=0),
                    preferred_element_type=F32,
                )

            if n >= 3:
                away[n - 3, rows, :] = multiply((1 - core) * 3 + n - 3)
            else:
                both = multiply(core * 3 + n)
                acc[2 * n, rows, :] = both[:, :128]
                acc[2 * n + 1, rows, :] = both[:, 128:]

    def ring(src, landing, dim, pieces):
        up, up_rank = occ_peer(me, dim, 1)
        down, down_rank = occ_peer(me, dim, 3)
        far, _ = occ_peer(me, dim, 2)

        def send(at, half, rank, slot):
            return [
                remote(src.at[pl.ds(begin, n)], landing.at[slot, pl.ds(to, n)], (rank, v))
                for begin, to, n in pieces(at, half)
            ]

        relays = send(far, 0, up_rank, 2) + send(far, 1, down_rank, 2)
        direct = send(up, 1, up_rank, 0) + send(down, 0, down_rank, 1)

        def forward():
            for c in relays:
                c.wait()
            for at, half in ((up, 0), (down, 1)):
                for begin, to, n in pieces(at, half):
                    src[pl.ds(begin, n), :] += landing[2, pl.ds(to, n), :]
            direct.extend(send(up, 0, up_rank, 0) + send(down, 1, down_rank, 1))

        def finish():
            for c in direct:
                c.wait()

        return forward, finish

    def of_y(at, half):
        return [(pl.multiple_of((at * 4 + 2 * half) * KEPT, 8), 2 * half * KEPT, 2 * KEPT)]

    def of_x(at, half):
        return [(pl.multiple_of((y * 4 + at) * KEPT, 8), y * KEPT, KEPT) for y in (2 * half, 2 * half + 1)]

    swap, first, second = [], [], []
    for n in (3, 4, 0, 5, 1, 2):
        product(n)
        if n >= 3:
            swap.append(remote(away.at[n - 3], other.at[n - 3], twin))
            continue
        swap[n].wait()

        @pl.loop(0, 16)
        def _(m):
            rows = pl.ds(pl.multiple_of(m * KEPT, 8), KEPT)
            acc[2 * n, rows, :] += other[n, rows, :128]
            acc[2 * n + 1, rows, :] += other[n, rows, 128:]

        first += [ring(acc.at[e], r1.at[e], "yx"[e % 2], (of_y, of_x)[e % 2]) for e in (2 * n, 2 * n + 1)]
        if n:
            first[2 * n - 2][0]()
            first[2 * n - 1][0]()
    first[4][0]()
    first[5][0]()

    for n in range(3):
        for e in (2 * n, 2 * n + 1):
            first[e][1]()
            for y in range(4):
                part = pl.ds(y * KEPT, KEPT)
                base = (me["y"] * 4 + y) if e % 2 == 0 else (y * 4 + me["x"])
                own = pl.ds(pl.multiple_of(base * KEPT, 8), KEPT)
                s1[e, part, :] = acc[e, own, :] + (r1[e, 0, part, :] + r1[e, 1, part, :])
            copies = []
            for k in range(1, 4):
                at, rank = occ_peer(me, "xy"[e % 2], k)
                rows = pl.ds(pl.multiple_of(at * KEPT, 8), KEPT)
                copies.append(remote(s1.at[e, rows], r2.at[e, k - 1], (rank, v)))
            second.append(copies)

    third = []
    for n in range(3):
        for h in range(2):
            e = 2 * n + h
            for c in second[e]:
                c.wait()
            own = pl.ds(pl.multiple_of(me["xy"[h]] * KEPT, 8), KEPT)
            s2[e] = (s1[e, own, :] + r2[e, 0]) + (r2[e, 1] + r2[e, 2])
            for half in range(2):
                if e % 3 == 2 - 2 * half:
                    continue
                to = e // 3 * 2 + half
                slot, k = e % 3 - half, lax.rem(zh - to + 4, 4)
                c = pltpu.make_async_remote_copy(
                    src_ref=s2.at[e],
                    dst_ref=r3.at[slot, lax.max(k - 1, 0)],
                    send_sem=ssem.at[sent[0]],
                    recv_sem=zsem.at[slot, lax.max(k - 1, 0)],
                    device_id=(r, to * 2 + core),
                    device_id_type=MESH,
                )
                sent[0] += 1
                third.append((to, c))
                pl.when(zh != to)(c.start)
    for to, c in third:
        pl.when(zh != to)(c.wait_send)
    total = s2[pl.ds(zh // 2 * 3 + lax.rem(zh, 2), 2)]
    for k in range(3):
        for slot in range(2):
            pltpu.make_async_remote_copy(
                src_ref=s2.at[slot], dst_ref=r3.at[slot, k], send_sem=ssem.at[0], recv_sem=zsem.at[slot, k],
                device_id=twin, device_id_type=MESH,
            ).wait_recv()
        total += r3[:, k]
    total = jnp.concatenate([total[0], total[1]], axis=1)
    mine[...] = jnp.where(lax.rem(zh, 2) == 0, total[:, :192], total[:, 64:])
    fourth = remote(mine, r4, beside)
    fourth.wait()
    u = mine[...] + r4[...]

    def kept(k, m):
        return u[27 * k - 1 + m : 27 * k + m]

    fifth = []
    for k in range(1, 8):
        ends[k - 1, :9] = jnp.concatenate([kept(e, 3 * k + t) for t in range(3) for e in (1, 2, 0)], axis=0)
        fifth.append(remote(ends.at[k - 1], r5.at[k - 1], triple(k)))
    for c in fifth:
        c.wait()
    turned = []
    for t in range(3):
        k = TURN.index(t)
        rows = [u[27 * k - 1 : 27 * k + 26]] if k else [kept(1, 2), u[0:26]]
        rows += [r5[6 - e, 3 * t : 3 * t + 3] for e in range(7)]
        turned.append(pltpu.roll(jnp.concatenate(rows, axis=0), 3 * q, 0))
    low = jnp.concatenate([turned[0], turned[1][:24]], axis=0)
    top = jnp.concatenate([turned[1][24:], turned[2]], axis=0)
    o_ref[...] = jnp.where(zl == 0, low, top)


def ladder(x, b):
    slabs = pltpu.VMEM((3, 4, 4, 2, SLAB, 128), F32)
    return pl.pallas_call(
        ladder_kernel,
        out_shape=jax.ShapeDtypeStruct((ROWS, 192), F32),
        in_specs=[pl.BlockSpec(memory_space=pl.ANY)] * 2,
        out_specs=pl.BlockSpec(memory_space=pltpu.VMEM),
        scratch_shapes=[
            pltpu.VMEM((3, THIRD, O, 384), F32),
            pltpu.VMEM((DEPTH, COLS), F32),
            pltpu.VMEM((8 * PITCH, 128), F32),
            slabs,
            slabs,
            slabs,
            pltpu.VMEM((4, 4, 2, 3, SLAB, 128), F32),
            pltpu.VMEM((PAIRS, 128), F32),
            pltpu.VMEM((UNIQUE, 512), BF16),
            pltpu.VMEM((UNIQUE, 512), BF16),
            pltpu.VMEM((UNIQUE, 128), BF16),
            pltpu.VMEM((6, DEPTH, 256), BF16),
            pltpu.VMEM((6, DEPTH, 256), BF16),
            pltpu.VMEM((3, UNIQUE, 256), F32),
            pltpu.VMEM((3, UNIQUE, 256), F32),
            pltpu.VMEM((6, UNIQUE, 128), F32),
            pltpu.VMEM((6, 3, 4 * KEPT, 128), F32),
            pltpu.VMEM((6, 4 * KEPT, 128), F32),
            pltpu.VMEM((6, 3, KEPT, 128), F32),
            pltpu.VMEM((6, KEPT, 128), F32),
            pltpu.VMEM((2, 3, KEPT, 128), F32),
            pltpu.VMEM((KEPT, 192), F32),
            pltpu.VMEM((KEPT, 192), F32),
            pltpu.VMEM((7, 16, 192), F32),
            pltpu.VMEM((7, 16, 192), F32),
            pltpu.SemaphoreType.DMA((154,)),
            pltpu.SemaphoreType.DMA((154,)),
            pltpu.SemaphoreType.DMA((27,)),
            pltpu.SemaphoreType.DMA((10,)),
            pltpu.SemaphoreType.DMA((2, 3)),
        ],
        compiler_params=pltpu.CompilerParams(collective_id=0, has_side_effects=True, vmem_limit_bytes=62 << 20),
    )(x, b)


def on_device(amplitudes, integrals):
    slab_matrix = integrals.transpose(1, 0, 2).reshape(DEPTH, COLS)
    return ladder(amplitudes, slab_matrix)


def solution(mesh):
    in_specs = (P("occ", "vir", None), P("vir", "occ", None))
    out_specs = P("occ", "vir")
    return jax.shard_map(
        on_device, mesh=mesh, in_specs=in_specs, out_specs=out_specs, check_vma=False
    )
```

```python
import jax
import jax.numpy as jnp
from jax import lax
from jax.experimental import pallas as pl
from jax.experimental.pallas import tpu as pltpu
from jax.sharding import PartitionSpec as P

O = 48
MESH = pl.DeviceIdType.MESH
F32, BF16 = jnp.float32, jnp.bfloat16
SIZE = {"y": 4, "x": 4, "z": 2}
AXIS = {"y": 0, "x": 1, "z": 2}
ORDERS = (("y", "x", "z"), ("x", "z", "y"), ("z", "y", "x"))
ROWS, DEPTH, COLS = 72, 576, 1536
PAIRS = 2304


def occ_place():
    r = lax.axis_index("occ")
    return {"y": r // 8, "x": lax.rem(r // 2, 4), "z": lax.rem(r, 2)}


def occ_peer(me, dim, k):
    c = dict(me)
    c[dim] = lax.rem(me[dim] + k, SIZE[dim])
    return c[dim], c["y"] * 8 + c["x"] * 2 + c["z"]


THIRD = ROWS // 3
BLOCK_AT = (0, 32, 72, 112)
SLAB = BLOCK_AT[3]
PITCH = 392

TURN = (2, 0, 1)
KEPT = 80
UNIQUE = 16 * KEPT
CHUNK = 640


def split(x):
    hi = x.astype(BF16)
    return hi, (x - hi.astype(F32)).astype(BF16)


def ladder_kernel(
    x_ref, b_any, o_ref,
    x, b_ref, turned, g0, g1, g2, g3, rest, s_hi, s_lo, s_mix, b_hi, b_lo,
    away, other, acc, r1, s1, r2, s2, r3, mine, r4, ends, r5,
    ssem, rsem, lsem, xsem, zsem,
):
    v = lax.axis_index("vir")
    r = lax.axis_index("occ")
    core, zh = lax.rem(v, 2), v // 2
    me = occ_place()
    q, zl = r // 2, me["z"]
    reads = {}
    for block in range(3):
        for t in range(3):
            rows = pl.ds(t * THIRD + block * 8, 8)
            reads[t, block] = pltpu.make_async_copy(
                x_ref.at[rows], x.at[t, pl.ds(block * 8, 8)], xsem.at[block * 3 + t]
            )
            reads[t, block].start()
    read_b = pltpu.make_async_copy(b_any, b_ref, xsem.at[9])

    def triple(k):
        return (lax.rem(q + k, 16) * 2 + zl, v)

    twin = (r, v + 1 - 2 * core)
    beside = (r + 1 - 2 * zl, v)
    devices = [twin, beside] + [triple(k) for k in range(1, 16)] + [(r, lax.rem(zh + k, 4) * 2 + core) for k in range(1, 4)]
    barrier = pltpu.get_barrier_semaphore()
    for d in devices:
        pl.semaphore_signal(barrier, inc=1, device_id=d, device_id_type=MESH)

    sent = [0, 0]

    def remote(src, dst, device):
        n = sent[0]
        sent[0] += 1
        c = pltpu.make_async_remote_copy(
            src_ref=src, dst_ref=dst, send_sem=ssem.at[n], recv_sem=rsem.at[n], device_id=device, device_id_type=MESH
        )
        c.start()
        return c

    lane = lax.broadcasted_iota(jnp.int32, (8, 128), 1)

    def regroup(t, block):
        @pl.loop(0, 8, unroll=8)
        def _(p):
            turned[pl.ds(pl.multiple_of(p * PITCH, 8), 384), 0:O] = x[t, block * 8 + p].T

        @pl.loop(0, 32, unroll=8)
        def _(to):
            at = (t, to // 8, lax.rem(to // 2, 4), lax.rem(to, 2))
            tiles = [jnp.zeros((8, 128), F32)] * 5
            for d in range(12):
                tile, off = d * O // 128, d * O % 128
                piece = turned[pl.ds(to * 12 + d, 8, stride=PITCH), :]
                if off:
                    piece = pltpu.roll(piece, off, 1)
                tiles[tile] = jnp.where((lane >= off) & (lane < off + O), piece, tiles[tile])
                if off + O > 128:
                    tiles[tile + 1] = jnp.where(lane < off + O - 128, piece, tiles[tile + 1])
            for n in range(4):
                g0[(*at, slice(BLOCK_AT[block] + 8 * n, BLOCK_AT[block] + 8 * n + 8))] = tiles[n]
            behind = (*at, slice(64, 72) if block < 2 else slice(104, 112))
            if block == 1:
                g0[behind] = jnp.where(lane < 64, g0[behind], pltpu.roll(tiles[4], 64, 1))
            else:
                g0[behind] = tiles[4]

    def view(ref, t, dim, at, rows):
        ix = [slice(None)] * 3
        ix[AXIS[dim]] = at
        if ref is g3:
            return ref.at[ix[0], ix[1], ix[2], t, rows]
        return ref.at[t, ix[0], ix[1], ix[2], rows]

    held = [g0, g1, g2, g3]

    def start(t, s, block):
        dim = ORDERS[t][s]
        rows = pl.ds(BLOCK_AT[block], BLOCK_AT[block + 1] - BLOCK_AT[block])
        src, dst = held[s], held[s + 1]
        copies = []
        for k in range(1, SIZE[dim]):
            at, rank = occ_peer(me, dim, k)
            copies.append(remote(view(src, t, dim, at, rows), view(dst, t, dim, me[dim], rows), (rank, v)))
        own = pltpu.make_async_copy(
            view(src, t, dim, me[dim], rows), view(dst, t, dim, me[dim], rows), lsem.at[sent[1]]
        )
        sent[1] += 1
        own.start()
        return copies + [own]

    flying = {}
    for block in range(3):
        for t in range(3):
            reads[t, block].wait()
            regroup(t, block)
            if block == t == 0:
                read_b.start()
                pl.semaphore_wait(barrier, len(devices))
            flying[t, block] = start(t, 0, block)

    def onward(s):
        for block in range(3):
            for t in range(3):
                for c in flying[t, block]:
                    c.wait()
                if s < 3:
                    flying[t, block] = start(t, s, block)

    onward(1)

    read_b.wait()

    @pl.loop(0, DEPTH // 48, unroll=2)
    def _(k):
        rows = pl.ds(pl.multiple_of(k * 48, 16), 48)
        b = b_ref[rows, :]
        for c in range(2):
            piece = jnp.concatenate([b[:, e * 384 + c * 192 : e * 384 + c * 192 + 192] for e in range(4)], axis=1)
            for n in range(3):
                b_hi[c * 3 + n, rows, :], b_lo[c * 3 + n, rows, :] = split(piece[:, n * 256 : (n + 1) * 256])

    onward(2)
    onward(3)

    flat = g3.reshape(32 * 3 * SLAB, 128)

    @pl.loop(0, PAIRS // THIRD, unroll=8)
    def _(g):
        both = flat[pl.ds(pl.multiple_of(g * SLAB + 64, 8), 8), :]
        rest[pl.ds(pl.multiple_of(g * THIRD, 8), 8), :] = both
        rest[pl.ds(pl.multiple_of(g * THIRD + 8, 8), 8), :] = pltpu.roll(both, 64, 1)
        rest[pl.ds(pl.multiple_of(g * THIRD + 16, 8), 8), :] = flat[pl.ds(pl.multiple_of(g * SLAB + 104, 8), 8), :]

    def place(t, p):
        return p // THIRD * SLAB + BLOCK_AT[p % THIRD // 8] + t * 8 + p % 8

    def straight(t, i, j, n):
        tiles = []
        for block in range(j // 8, (j + n + 7) // 8):
            p = i * O + block % 6 * 8
            tiles.append(rest[p : p + 8, :] if t == 4 else flat[pl.ds(place(t, p), 8), :])
        return jnp.concatenate(tiles, axis=0)[j % 8 : j % 8 + n]

    def mirrored(t, i, j, n):
        parts = []
        for first, count in ((j, min(n, O - j)), (0, n - min(n, O - j))):
            if count and t == 4:
                parts.append(rest[pl.ds(first * O + i, count, stride=O), :])
            elif count:
                parts.append(flat[pl.ds(place(t, first * O + i), count, stride=2 * SLAB), :])
        return jnp.concatenate(parts, axis=0)

    for t in range(5):
        for own in range(16):
            sums = []
            for k in range(3):
                i, m = 3 * own + TURN[k], int(k == 0)
                sums.append(straight(t, i, 3 * own + m, 27 - m) + mirrored(t, i, 3 * own + m, 27 - m))
            total = jnp.concatenate(sums, axis=0)
            at, lanes = slice(own * KEPT, (own + 1) * KEPT), slice(t * 128, (t + 1) * 128)
            if t < 4:
                s_hi[at, lanes], s_lo[at, lanes] = split(total)
            else:
                high = total.astype(BF16).astype(F32)
                low = pltpu.roll(total - high, 64, 1)
                left = lax.broadcasted_iota(jnp.int32, total.shape, 1) < 64
                s_mix[at, :] = jnp.where(left, high, low).astype(BF16)


    def product(n):
        @pl.loop(0, UNIQUE // CHUNK)
        def _(m):
            rows = pl.ds(pl.multiple_of(m * CHUNK, 128), CHUNK)

            def multiply(at):
                hi, lo, mix = s_hi[rows, :], s_lo[rows, :], s_mix[rows, :]
                hi_top, hi_end = b_hi[at, :512], b_hi[at, 512:]
                lo_top, lo_end = b_lo[at, :512], b_lo[at, 512:]
                none = jnp.zeros_like(lo_end)
                return jnp.dot(
                    jnp.concatenate([hi, mix, lo, hi, mix], axis=1),
                    jnp.concatenate([hi_top, hi_end, hi_end, hi_top, lo_top, lo_end, none], axis=0),
                    preferred_element_type=F32,
                )

            if n >= 3:
                away[n - 3, rows, :] = multiply((1 - core) * 3 + n - 3)
            else:
                both = multiply(core * 3 + n)
                acc[2 * n, rows, :] = both[:, :128]
                acc[2 * n + 1, rows, :] = both[:, 128:]

    def ring(src, landing, dim, pieces):
        up, up_rank = occ_peer(me, dim, 1)
        down, down_rank = occ_peer(me, dim, 3)
        far, _ = occ_peer(me, dim, 2)

        def send(at, half, rank, slot):
            return [
                remote(src.at[pl.ds(begin, n)], landing.at[slot, pl.ds(to, n)], (rank, v))
                for begin, to, n in pieces(at, half)
            ]

        relays = send(far, 0, up_rank, 2) + send(far, 1, down_rank, 2)
        direct = send(up, 1, up_rank, 0) + send(down, 0, down_rank, 1)

        def forward():
            for c in relays:
                c.wait()
            for at, half in ((up, 0), (down, 1)):
                for begin, to, n in pieces(at, half):
                    src[pl.ds(begin, n), :] += landing[2, pl.ds(to, n), :]
            direct.extend(send(up, 0, up_rank, 0) + send(down, 1, down_rank, 1))

        def finish():
            for c in direct:
                c.wait()

        return forward, finish

    def of_y(at, half):
        return [(pl.multiple_of((at * 4 + 2 * half) * KEPT, 8), 2 * half * KEPT, 2 * KEPT)]

    def of_x(at, half):
        return [(pl.multiple_of((y * 4 + at) * KEPT, 8), y * KEPT, KEPT) for y in (2 * half, 2 * half + 1)]

    swap, first, second = [], [], []
    for n in (3, 4, 0, 5, 1, 2):
        product(n)
        if n >= 3:
            swap.append(remote(away.at[n - 3], other.at[n - 3], twin))
            continue
        swap[n].wait()

        @pl.loop(0, 16, unroll=4)
        def _(m):
            rows = pl.ds(pl.multiple_of(m * KEPT, 8), KEPT)
            acc[2 * n, rows, :] += other[n, rows, :128]
            acc[2 * n + 1, rows, :] += other[n, rows, 128:]

        first += [ring(acc.at[e], r1.at[e], "yx"[e % 2], (of_y, of_x)[e % 2]) for e in (2 * n, 2 * n + 1)]
        if n:
            first[2 * n - 2][0]()
            first[2 * n - 1][0]()
    first[4][0]()
    first[5][0]()

    for n in range(3):
        for e in (2 * n, 2 * n + 1):
            first[e][1]()
            for y in range(4):
                part = pl.ds(y * KEPT, KEPT)
                base = (me["y"] * 4 + y) if e % 2 == 0 else (y * 4 + me["x"])
                own = pl.ds(pl.multiple_of(base * KEPT, 8), KEPT)
                s1[e, part, :] = acc[e, own, :] + (r1[e, 0, part, :] + r1[e, 1, part, :])
            copies = []
            for k in range(1, 4):
                at, rank = occ_peer(me, "xy"[e % 2], k)
                rows = pl.ds(pl.multiple_of(at * KEPT, 8), KEPT)
                copies.append(remote(s1.at[e, rows], r2.at[e, k - 1], (rank, v)))
            second.append(copies)

    third = []
    for n in range(3):
        for h in range(2):
            e = 2 * n + h
            for c in second[e]:
                c.wait()
            own = pl.ds(pl.multiple_of(me["xy"[h]] * KEPT, 8), KEPT)
            s2[e] = (s1[e, own, :] + r2[e, 0]) + (r2[e, 1] + r2[e, 2])
            for half in range(2):
                if e % 3 == 2 - 2 * half:
                    continue
                to = e // 3 * 2 + half
                slot, k = e % 3 - half, lax.rem(zh - to + 4, 4)
                c = pltpu.make_async_remote_copy(
                    src_ref=s2.at[e],
                    dst_ref=r3.at[slot, lax.max(k - 1, 0)],
                    send_sem=ssem.at[sent[0]],
                    recv_sem=zsem.at[slot, lax.max(k - 1, 0)],
                    device_id=(r, to * 2 + core),
                    device_id_type=MESH,
                )
                sent[0] += 1
                third.append((to, c))
                pl.when(zh != to)(c.start)
    for to, c in third:
        pl.when(zh != to)(c.wait_send)
    total = s2[pl.ds(zh // 2 * 3 + lax.rem(zh, 2), 2)]
    for k in range(3):
        for slot in range(2):
            pltpu.make_async_remote_copy(
                src_ref=s2.at[slot], dst_ref=r3.at[slot, k], send_sem=ssem.at[0], recv_sem=zsem.at[slot, k],
                device_id=twin, device_id_type=MESH,
            ).wait_recv()
        total += r3[:, k]
    total = jnp.concatenate([total[0], total[1]], axis=1)
    mine[...] = jnp.where(lax.rem(zh, 2) == 0, total[:, :192], total[:, 64:])
    fourth = remote(mine, r4, beside)
    fourth.wait()
    u = mine[...] + r4[...]

    def kept(k, m):
        return u[27 * k - 1 + m : 27 * k + m]

    fifth = []
    for k in range(1, 8):
        ends[k - 1, :9] = jnp.concatenate([kept(e, 3 * k + t) for t in range(3) for e in (1, 2, 0)], axis=0)
        fifth.append(remote(ends.at[k - 1], r5.at[k - 1], triple(k)))
    for c in fifth:
        c.wait()
    turned = []
    for t in range(3):
        k = TURN.index(t)
        rows = [u[27 * k - 1 : 27 * k + 26]] if k else [kept(1, 2), u[0:26]]
        rows += [r5[6 - e, 3 * t : 3 * t + 3] for e in range(7)]
        turned.append(pltpu.roll(jnp.concatenate(rows, axis=0), 3 * q, 0))
    low = jnp.concatenate([turned[0], turned[1][:24]], axis=0)
    top = jnp.concatenate([turned[1][24:], turned[2]], axis=0)
    o_ref[...] = jnp.where(zl == 0, low, top)


def ladder(x, b):
    slabs = pltpu.VMEM((3, 4, 4, 2, SLAB, 128), F32)
    return pl.pallas_call(
        ladder_kernel,
        out_shape=jax.ShapeDtypeStruct((ROWS, 192), F32),
        in_specs=[pl.BlockSpec(memory_space=pl.ANY)] * 2,
        out_specs=pl.BlockSpec(memory_space=pltpu.VMEM),
        scratch_shapes=[
            pltpu.VMEM((3, THIRD, O, 384), F32),
            pltpu.VMEM((DEPTH, COLS), F32),
            pltpu.VMEM((8 * PITCH, 128), F32),
            slabs,
            slabs,
            slabs,
            pltpu.VMEM((4, 4, 2, 3, SLAB, 128), F32),
            pltpu.VMEM((PAIRS, 128), F32),
            pltpu.VMEM((UNIQUE, 512), BF16),
            pltpu.VMEM((UNIQUE, 512), BF16),
            pltpu.VMEM((UNIQUE, 128), BF16),
            pltpu.VMEM((6, DEPTH, 256), BF16),
            pltpu.VMEM((6, DEPTH, 256), BF16),
            pltpu.VMEM((3, UNIQUE, 256), F32),
            pltpu.VMEM((3, UNIQUE, 256), F32),
            pltpu.VMEM((6, UNIQUE, 128), F32),
            pltpu.VMEM((6, 3, 4 * KEPT, 128), F32),
            pltpu.VMEM((6, 4 * KEPT, 128), F32),
            pltpu.VMEM((6, 3, KEPT, 128), F32),
            pltpu.VMEM((6, KEPT, 128), F32),
            pltpu.VMEM((2, 3, KEPT, 128), F32),
            pltpu.VMEM((KEPT, 192), F32),
            pltpu.VMEM((KEPT, 192), F32),
            pltpu.VMEM((7, 16, 192), F32),
            pltpu.VMEM((7, 16, 192), F32),
            pltpu.SemaphoreType.DMA((154,)),
            pltpu.SemaphoreType.DMA((154,)),
            pltpu.SemaphoreType.DMA((27,)),
            pltpu.SemaphoreType.DMA((10,)),
            pltpu.SemaphoreType.DMA((2, 3)),
        ],
        compiler_params=pltpu.CompilerParams(collective_id=0, has_side_effects=True, vmem_limit_bytes=62 << 20),
    )(x, b)


def on_device(amplitudes, integrals):
    slab_matrix = integrals.transpose(1, 0, 2).reshape(DEPTH, COLS)
    return ladder(amplitudes, slab_matrix)


def solution(mesh):
    in_specs = (P("occ", "vir", None), P("vir", "occ", None))
    out_specs = P("occ", "vir")
    return jax.shard_map(
        on_device, mesh=mesh, in_specs=in_specs, out_specs=out_specs, check_vma=False
    )
```
